256 devices in a mesh: stratum: 16 (over x, y_lo, core), group: 16 (over z, y_hi).
Axes of the slice: x: 4, y: 4 (y_hi: 2, y_lo: 2; y = y_hi * 2 + y_lo), z: 8, core: 2. Of those that a mesh axis runs over, the one named last changes fastest.
Arguments:
- row_factors: bfloat16 [262144, 256], P(('stratum', 'group')), may hold values from -0.59765625 to 0.59765625
- row_bias: bfloat16 [262144], P(('stratum', 'group')), may hold values from -4 to 4
- row_sums: float32 [262144, 256], P(('stratum', 'group')), may hold values from 5 to 500
- row_bias_sums: float32 [262144], P(('stratum', 'group')), may hold values from 100000 to 100000000
- col_factors: bfloat16 [32768, 256], P(('stratum', 'group')), may hold values from -0.59765625 to 0.59765625
- col_bias: bfloat16 [32768], P(('stratum', 'group')), may hold values from -4 to 4
- col_sums: float32 [32768, 256], P(('stratum', 'group')), may hold values from 5 to 500
- col_bias_sums: float32 [32768], P(('stratum', 'group')), may hold values from 100 to 100000000
- row_pick: int32 [16, 16, 2, 512], P('stratum', 'group'), may hold values from 0 to 1023, as said below
- counts: int32 [16, 16, 2, 512, 2048], P('stratum', 'group'), may hold values from 0 to 1024, as said below
Outputs:
- row_factors_out: bfloat16 [262144, 256], P(('stratum', 'group'))
- row_bias_out: bfloat16 [262144], P(('stratum', 'group'))
- row_sums_out: float32 [262144, 256], P(('stratum', 'group'))
- row_bias_sums_out: float32 [262144], P(('stratum', 'group'))
- col_factors_out: bfloat16 [32768, 256], P(('stratum', 'group'))
- col_bias_out: bfloat16 [32768], P(('stratum', 'group'))
- col_sums_out: float32 [32768, 256], P(('stratum', 'group'))
- col_bias_sums_out: float32 [32768], P(('stratum', 'group'))
The draws below stay inside these ranges and needn't reach their ends.
Inputs may be any that keep to these rules, and one draw needn't show every extreme that they name: `row_pick`: the 512 indices of one device in one stratum are distinct. About three fifths of the counts are nonzero.
All inputs are finite; a program needn't handle non-finite values.
Results may differ from the reference program's by a relative error of at most 0.00175.
The reference program's roundings to bfloat16 on the way (of `residual_half`) count: a program that leaves them out, or rounds other values in their place, can miss the bound.
Values may be sent and summed in bfloat16 or wider, within the bound.
No kernel may reach another device: no remote copies, remote signals or barrier semaphores. Data moves between devices by JAX's collectives and lax.ppermute only.
A program may use at most 128 MiB of HBM per device.

```python
import math
import jax
import jax.numpy as jnp
from jax import lax

K = 256
BATCH = 512
STEPS = 2
RTAB = 1024
C_BLK = 2048
ROWS = 262144
COLS = 32768
N_STRATUM = 16
N_GROUP = 16


def draw_row_pick(key, part):
    key = jax.random.fold_in(key, 11)
    subkeys = jax.random.split(key, N_STRATUM * N_GROUP * STEPS)
    picks = jax.vmap(lambda subkey: jax.random.permutation(subkey, RTAB)[:BATCH])(subkeys)
    return picks.reshape(N_STRATUM, N_GROUP, STEPS, BATCH).astype(jnp.int32)


def draw_counts(key, part):
    key = jax.random.fold_in(key, 23)
    key_live, key_scale, key_value = jax.random.split(key, 3)
    shape = (N_STRATUM, N_GROUP, STEPS, BATCH, C_BLK)
    live = jax.random.randint(key_live, shape, 0, 5) < 3
    exponent = jax.random.randint(key_scale, shape, 0, 11)
    ceiling = jnp.left_shift(jnp.ones(shape, jnp.int32), exponent)
    value = jax.random.randint(key_value, shape, 1, ceiling + 1)
    return jnp.where(live, value, 0).astype(jnp.int32)


def steps_of(rng, extent, pieces, least, top_value):
    factor_of, own = 1.0, jax.random.fold_in(rng, 6)
    for axis_at, shards_of in pieces:
        heights = jnp.exp(jax.random.uniform(jax.random.fold_in(own, axis_at), (shards_of,), jnp.float32, least / len(pieces), top_value / len(pieces)))
        factor_of = factor_of * jnp.repeat(heights, extent[axis_at] // shards_of).reshape([-1 if axis == axis_at else 1 for axis in range(len(extent))])
    return factor_of


def normal_values(key, dims, width, reach, pieces=(), kind=jnp.bfloat16):
    gain = steps_of(key, dims, pieces, -0.22, 0.18) if pieces else 1.0
    drawn = jax.random.normal(key, dims, jnp.float32) * width * gain
    return jnp.minimum(jnp.maximum(drawn, -reach), reach).astype(kind)


def setup_inputs(seed: int = 0) -> dict:
    arg_keys = jax.random.split(jax.random.key(seed), 11)
    return {
        "row_factors": normal_values(arg_keys[0], (ROWS, K), 0.1, 0.59765625, ((0, 256),)),
        "row_bias": normal_values(arg_keys[1], (ROWS,), 1.0, 4.0, ((0, 256),)),
        "row_sums": jnp.clip(jnp.exp(math.log(500.0) - 4.6051702 * jax.random.uniform(arg_keys[2], (ROWS, K), jnp.float32) ** steps_of(arg_keys[2], (ROWS, K), ((0, 256),), -0.2, 0.2)), 5.0, 500.0),
        "row_bias_sums": jnp.clip(jnp.exp(math.log(100000000) - 6.9077553 * jax.random.uniform(arg_keys[3], (ROWS,), jnp.float32) ** steps_of(arg_keys[3], (ROWS,), ((0, 256),), -0.2, 0.2)), 100000.0, 100000000),
        "col_factors": normal_values(arg_keys[4], (COLS, K), 0.1, 0.59765625, ((0, 256),)),
        "col_bias": normal_values(arg_keys[5], (COLS,), 1.0, 4.0, ((0, 256),)),
        "col_sums": jnp.clip(jnp.exp(math.log(500.0) - 4.6051702 * jax.random.uniform(arg_keys[6], (COLS, K), jnp.float32) ** steps_of(arg_keys[6], (COLS, K), ((0, 256),), -0.2, 0.2)), 5.0, 500.0),
        "col_bias_sums": jnp.clip(jnp.exp(math.log(100000000) - 13.815511 * jax.random.uniform(arg_keys[7], (COLS,), jnp.float32) ** steps_of(arg_keys[7], (COLS,), ((0, 256),), -0.2, 0.2)), 100.0, 100000000),
        "row_pick": draw_row_pick(jax.random.fold_in(arg_keys[10], 71), 0),
        "counts": draw_counts(jax.random.fold_in(arg_keys[10], 71), 0),
    }


LEARN_RATE = 0.2
COUNT_CAP = 100.0
POWER = 0.75

def weighted_residual(picked, picked_bias, column_block, column_bias, count_tile):
    scores = jnp.dot(picked, column_block.T, preferred_element_type=jnp.float32)
    scores = scores + picked_bias.astype(jnp.float32)[:, None] + column_bias.astype(jnp.float32)[None, :]
    counted = count_tile.astype(jnp.float32)
    target = jnp.log(jnp.maximum(counted, 1.0))
    weight = jnp.minimum((counted / COUNT_CAP) ** POWER, 1.0)
    return weight * (scores - target)

def adagrad(parameter, running, gradient):
    new_running = running + gradient * gradient
    updated = parameter.astype(jnp.float32) - LEARN_RATE * gradient / jnp.sqrt(new_running)
    return (updated.astype(parameter.dtype), new_running)

def device_rows(row_table, table_bias, table_sums, table_bias_sums, pick, count_tile, column_block, column_bias):
    picked = row_table[pick]
    picked_bias = table_bias[pick]
    residual = weighted_residual(picked, picked_bias, column_block, column_bias, count_tile)
    residual_half = residual.astype(jnp.bfloat16)
    row_grad = jnp.dot(residual_half, column_block, preferred_element_type=jnp.float32)
    row_bias_grad = lax.optimization_barrier(jnp.sum(residual, axis=1))
    col_grad = lax.dot_general(residual_half, picked, (((0,), (0,)), ((), ())), preferred_element_type=jnp.float32)
    col_bias_grad = lax.optimization_barrier(jnp.sum(residual, axis=0))
    new_picked, new_sums = adagrad(picked, table_sums[pick], row_grad)
    new_bias, new_bias_sums = adagrad(picked_bias, table_bias_sums[pick], row_bias_grad)
    tables = (row_table.at[pick].set(new_picked), table_bias.at[pick].set(new_bias), table_sums.at[pick].set(new_sums), table_bias_sums.at[pick].set(new_bias_sums))
    return (tables, col_grad, col_bias_grad)

def per_device(values):
    return values.reshape((N_STRATUM, N_GROUP, RTAB) + values.shape[1:])

def reference(row_factors, row_bias, row_sums, row_bias_sums, col_factors, col_bias, col_sums, col_bias_sums, row_pick, counts):
    tables = tuple((per_device(values) for values in (row_factors, row_bias, row_sums, row_bias_sums)))
    held = tuple((values.reshape((N_STRATUM, C_BLK) + values.shape[1:]) for values in (col_factors, col_bias, col_sums, col_bias_sums)))
    for substep in range(STEPS):

        def stratum_work(inputs):
            tables_here, pick_stack, tile_stack, column_block, column_bias = inputs

            def group_work(running, member):
                updated, col_grad, col_bias_grad = device_rows(member[0], member[1], member[2], member[3], member[4], member[5], column_block, column_bias)
                return ((running[0] + col_grad, running[1] + col_bias_grad), updated)
            initial = (jnp.zeros((C_BLK, K), jnp.float32), jnp.zeros((C_BLK,), jnp.float32))
            totals, updated = lax.scan(group_work, initial, tables_here + (pick_stack, tile_stack))
            return (updated, totals)
        updated, totals = lax.map(stratum_work, (tables, row_pick[:, :, substep], counts[:, :, substep], held[0], held[1]))
        tables = updated
        new_factors, new_sums = adagrad(held[0], held[2], totals[0])
        new_bias, new_bias_sums = adagrad(held[1], held[3], totals[1])
        held = tuple((jnp.roll(values, 1, axis=0) for values in (new_factors, new_bias, new_sums, new_bias_sums)))
    row_outs = tuple((values.reshape((ROWS,) + values.shape[3:]) for values in tables))
    col_outs = tuple((values.reshape((COLS,) + values.shape[2:]) for values in held))
    return (row_outs[0], row_outs[1], row_outs[2], row_outs[3], col_outs[0], col_outs[1], col_outs[2], col_outs[3])
```

```python
import functools

import jax
import jax.numpy as jnp
from jax import lax
from jax.experimental import pallas as pl
from jax.experimental.pallas import tpu as pltpu
from jax.sharding import PartitionSpec as P

LEARN_RATE = 0.2
COUNT_CAP = 100.0
POWER = 0.75

K = 256
BATCH = 512
RTAB = 1024
SHARD = 128
PIECE = 256
PIECE_B = PIECE + 16
PIECE_F = PIECE + 8
SHARD_B = SHARD + 16
SHARD_F = SHARD + 8
TOP = 144
TOP_F = 136
NZ = 8
NY = 2

F32 = jnp.float32
BF16 = jnp.bfloat16
VMEM = pl.BlockSpec(memory_space=pltpu.VMEM)
SMEM = pl.BlockSpec(memory_space=pltpu.SMEM)


def call(kernel, out_shape, flops=0, size=0, specs=None, n_in=0):
    return pl.pallas_call(
        kernel,
        out_shape=out_shape,
        in_specs=specs or [VMEM] * n_in,
        out_specs=jax.tree.map(lambda _: VMEM, out_shape),
        cost_estimate=pl.CostEstimate(flops=flops, bytes_accessed=size, transcendentals=0),
        compiler_params=pltpu.CompilerParams(vmem_limit_bytes=32 * 1024 * 1024),
    )


def shape(dims, dtype):
    return jax.ShapeDtypeStruct(dims, dtype)


def along_z(block, distance):
    route = [(g, ((g // NY + distance) % NZ) * NY + g % NY) for g in range(NZ * NY)]
    return lax.ppermute(block, "group", route)


def swap_y(block):
    return lax.ppermute(block, "group", [(g, g ^ 1) for g in range(NZ * NY)])


def next_stratum(block):
    size = lax.axis_size("stratum")
    return lax.ppermute(block, "stratum", [(s, (s + 1) % size) for s in range(size)])


def next_stratum_swap_y(block):
    size = lax.axis_size("stratum")
    group = NZ * NY
    route = [
        (s * group + g, ((s + 1) % size) * group + (g ^ 1)) for s in range(size) for g in range(group)
    ]
    return lax.ppermute(block, ("stratum", "group"), route)


def pack_kernel(rows_ref, bias_ref, out_ref):
    out_ref[:SHARD] = rows_ref[...]
    pad = out_ref.shape[0] - SHARD
    out_ref[SHARD:] = jnp.zeros((pad, K), out_ref.dtype)
    wide = jnp.concatenate([bias_ref[...], bias_ref[...]], axis=1).astype(F32)
    row = lax.broadcasted_iota(jnp.int32, (pad, K), 0)
    out_ref[SHARD:] = jnp.where(row == 0, jnp.broadcast_to(wide, (pad, K)), 0.0).astype(out_ref.dtype)


def pack(rows, bias):
    pad = 16 if rows.dtype == BF16 else 8
    return call(pack_kernel, shape((SHARD + pad, K), rows.dtype), n_in=2)(rows, bias.reshape(1, SHARD))


def merge_kernel(y_ref, own_ref, other_ref, out_ref):
    y = y_ref[0]
    mine = pl.multiple_of(y * SHARD, SHARD)
    theirs = pl.multiple_of((1 - y) * SHARD, SHARD)
    out_ref[pl.ds(mine, SHARD)] = own_ref[:SHARD]
    out_ref[pl.ds(theirs, SHARD)] = other_ref[:SHARD]
    a = own_ref[SHARD:].astype(F32)
    b = other_ref[SHARD:].astype(F32)
    lane = lax.broadcasted_iota(jnp.int32, a.shape, 1)
    out_ref[PIECE:] = jnp.where((lane < SHARD) == (y == 0), a, b).astype(out_ref.dtype)


def merge(y, own, other):
    pad = own.shape[0] - SHARD
    return call(
        merge_kernel, shape((PIECE + pad, K), own.dtype), specs=[SMEM, VMEM, VMEM]
    )(y, own, other)


def pick_rows(table, bias, pick_col, picked_ref, picked_bias_ref):
    lane = lax.broadcasted_iota(jnp.int32, (BATCH, RTAB), 1)
    hot = lane == pick_col
    one_hot = jnp.where(hot, 1.0, 0.0).astype(BF16)
    picked_ref[...] = jnp.dot(one_hot, table, preferred_element_type=F32).astype(BF16)
    column = jnp.sum(jnp.where(hot, bias, 0.0), axis=1, keepdims=True)
    picked_bias_ref[...] = jnp.broadcast_to(column, (BATCH, 128))


def gather_kernel(table_ref, bias_ref, pick_col_ref, picked_ref, picked_bias_ref):
    pick_rows(
        table_ref[...], bias_ref[...].astype(F32), pick_col_ref[:, :1], picked_ref, picked_bias_ref
    )


PICKED = (shape((BATCH, K), BF16), shape((BATCH, 128), F32))


def gather(table, bias, pick_col):
    return call(gather_kernel, PICKED, flops=2 * BATCH * RTAB * K, size=1 << 20, n_in=3)(
        table, bias, pick_col
    )


def row_update_kernel(
    step,
    grad_refs,
    bias_grad_refs,
    table_ref,
    bias_ref,
    sums_ref,
    bias_sums_ref,
    pick_col_ref,
    pick_row_ref,
    table_out,
    bias_out,
    sums_out,
    bias_sums_out,
    *picked_refs,
):
    grad = grad_refs[...]
    high = grad.astype(BF16)
    rest = grad - high.astype(F32)
    middle = rest.astype(BF16)
    low = (rest - middle.astype(F32)).astype(BF16)
    parts = jnp.concatenate([high, middle, low], axis=1)
    chunk = 256
    for c in range(RTAB // chunk):
        rows = slice(c * chunk, (c + 1) * chunk)
        index = lax.broadcasted_iota(jnp.int32, (chunk, BATCH), 0) + c * chunk
        spread = jnp.where(index == pick_row_ref[step : step + 1, :], 1.0, 0.0).astype(BF16)
        moved = jnp.dot(spread, parts, preferred_element_type=F32)
        full = moved[:, :K] + moved[:, K : 2 * K] + moved[:, 2 * K :]
        new_sums = sums_ref[rows] + full * full
        sums_out[rows] = new_sums
        table_out[rows] = (
            table_ref[rows].astype(F32) - LEARN_RATE * full * lax.rsqrt(new_sums)
        ).astype(BF16)
    column = jnp.sum(bias_grad_refs[...], axis=1, keepdims=True)
    lane = lax.broadcasted_iota(jnp.int32, (BATCH, RTAB), 1)
    hot = lane == pick_col_ref[:, step : step + 1]
    bias_grad = jnp.sum(jnp.where(hot, column, 0.0), axis=0, keepdims=True)
    new_bias_sums = bias_sums_ref[...] + bias_grad * bias_grad
    bias_sums_out[...] = new_bias_sums
    new_bias = (
        bias_ref[...].astype(F32) - LEARN_RATE * bias_grad * lax.rsqrt(new_bias_sums)
    ).astype(BF16)
    bias_out[...] = new_bias
    if picked_refs:
        pick_rows(
            table_out[...], new_bias.astype(F32), pick_col_ref[:, step + 1 : step + 2], *picked_refs
        )


def row_update(step, last, grad, bias_grad, table, bias, sums, bias_sums, pick_col, pick_row):
    outs = (
        shape((RTAB, K), BF16),
        shape((1, RTAB), BF16),
        shape((RTAB, K), F32),
        shape((1, RTAB), F32),
    )
    if not last:
        outs = outs + PICKED
    return call(
        functools.partial(row_update_kernel, step),
        outs,
        flops=8 * BATCH * RTAB * K,
        size=5 << 20,
        n_in=8,
    )(grad, bias_grad, table, bias, sums, bias_sums, pick_col, pick_row)


def tile_kernel(n, split, first, *refs):
    refs = list(refs)
    refs.pop(0)
    picked_ref, picked_bias_ref = refs.pop(0), refs.pop(0)
    columns = [refs.pop(0) for _ in range(n + (1 if split else 0))]
    counts = [refs.pop(0) for _ in range(n)]
    if not first:
        grad_in, bias_in = refs.pop(0), refs.pop(0)
    partial_refs = [refs.pop(0) for _ in range(n)]
    grad_out, bias_out = refs
    picked = picked_ref[...]
    picked_bias = jnp.concatenate([picked_bias_ref[...]] * 2, axis=1)
    row_grad = None if first else grad_in[...]
    row_bias_grad = None if first else bias_in[...]
    for i in range(n):
        if split and i == n - 1:
            top, bottom = columns[n - 1], columns[n]
            block = jnp.concatenate([top[...], bottom[: PIECE - TOP]], axis=0)
            tail = bottom[PIECE - TOP :]
        else:
            block, tail = columns[i][:PIECE], columns[i][PIECE:]
        bias = tail.astype(F32)[:1]
        scores = lax.dot_general(
            picked, block, (((1,), (1,)), ((), ())), preferred_element_type=F32
        )
        scores = scores + picked_bias + bias
        counted = counts[i][...].astype(F32)
        target = jnp.log(jnp.maximum(counted, 1.0))
        weight = jnp.exp(POWER * target - POWER * jnp.log(jnp.float32(COUNT_CAP)))
        weight = jnp.where(counted > 0.0, jnp.minimum(weight, 1.0), 0.0)
        residual = weight * (scores - target)
        half = residual.astype(BF16)
        part = jnp.dot(half, block, preferred_element_type=F32)
        row_grad = part if row_grad is None else row_grad + part
        lanes = residual[:, :128] + residual[:, 128:]
        row_bias_grad = lanes if row_bias_grad is None else row_bias_grad + lanes
        partial_refs[i][:PIECE] = lax.dot_general(
            half, picked, (((0,), (0,)), ((), ())), preferred_element_type=F32
        )
        bias_grad = jnp.sum(residual, axis=0, keepdims=True)
        row = lax.broadcasted_iota(jnp.int32, (PIECE_F - PIECE, K), 0)
        partial_refs[i][PIECE:] = jnp.where(row == 0, bias_grad, 0.0)
    grad_out[...] = row_grad
    bias_out[...] = row_bias_grad


def tiles(step, offsets, ids, picked, columns, counts, grads, split=False):
    n = len(offsets)
    first = grads is None

    def whole(dims):
        return pl.BlockSpec(dims, lambda i, ids: (0, 0))

    specs = [whole((BATCH, K)), whole((BATCH, 128))]
    specs += [whole(c.shape) for c in columns]
    for offset in offsets:
        specs.append(
            pl.BlockSpec(
                (None, None, None, BATCH, PIECE),
                functools.partial(lambda at, i, ids: (0, 0, step, 0, ids[at]), offset % NZ),
            )
        )
    args = [*picked, *columns, *([counts] * n)]
    if not first:
        specs += [whole((BATCH, K)), whole((BATCH, 128))]
        args += list(grads)
    out_specs = [whole((PIECE_F, K))] * n + [whole((BATCH, K)), whole((BATCH, 128))]
    out_shape = [shape((PIECE_F, K), F32)] * n + [shape((BATCH, K), F32), shape((BATCH, 128), F32)]
    outs = pl.pallas_call(
        functools.partial(tile_kernel, n, split, first),
        grid_spec=pltpu.PrefetchScalarGridSpec(
            num_scalar_prefetch=1, grid=(1,), in_specs=specs, out_specs=out_specs
        ),
        out_shape=out_shape,
        cost_estimate=pl.CostEstimate(
            flops=n * 6 * BATCH * PIECE * K,
            bytes_accessed=n * (BATCH * PIECE * 4 + PIECE * K * 6),
            transcendentals=2 * n * BATCH * PIECE,
        ),
        compiler_params=pltpu.CompilerParams(vmem_limit_bytes=40 * 1024 * 1024),
    )(ids, *args)
    return dict(zip(offsets, outs[:n])), tuple(outs[n:])


def relay_kernel(up_ref, down_ref, up3_ref, down3_ref, up4_ref, down4_ref, up_out, down_out):
    up_out[:TOP_F] = up_ref[:TOP_F] + up3_ref[:TOP_F] + up4_ref[...]
    up_out[TOP_F:] = up_ref[TOP_F:] + up3_ref[TOP_F:]
    down_out[:TOP_F] = down_ref[:TOP_F] + down3_ref[:TOP_F]
    down_out[TOP_F:] = down_ref[TOP_F:] + down3_ref[TOP_F:] + down4_ref[...]


def split_sum_kernel(y_ref, *refs):
    parts, (own_out, other_out) = refs[:-2], refs[-2:]
    y = y_ref[0]
    mine = pl.multiple_of(y * SHARD, SHARD)
    theirs = pl.multiple_of((1 - y) * SHARD, SHARD)
    own_out[:SHARD] = sum(p[pl.ds(mine, SHARD)] for p in parts[1:]) + parts[0][pl.ds(mine, SHARD)]
    other_out[:SHARD] = (
        sum(p[pl.ds(theirs, SHARD)] for p in parts[1:]) + parts[0][pl.ds(theirs, SHARD)]
    )
    tail = parts[0][PIECE:] + sum(p[PIECE:] for p in parts[1:])
    low, high = tail[:, :SHARD], tail[:, SHARD:]
    first = jnp.concatenate([low, low], axis=1)
    second = jnp.concatenate([high, high], axis=1)
    own_out[SHARD:] = jnp.where(y == 0, first, second)
    other_out[SHARD:] = jnp.where(y == 0, second, first)


def gather_columns(own):
    up1, down1 = along_z(own, -1), along_z(own, 1)
    up2, down2 = along_z(own, -2), along_z(own, 2)
    up3, down3 = along_z(up2, -1), along_z(down2, 1)
    top4, bottom4 = along_z(up2[:TOP], -2), along_z(down2[TOP:], 2)
    return {0: own, 1: up1, -1: down1, 2: up2, -2: down2, 3: up3, -3: down3, 4: (top4, bottom4)}


def reduce_columns(part):
    up3, down3 = along_z(part[3], 1), along_z(part[-3], -1)
    up4, down4 = along_z(part[4][:TOP_F], 2), along_z(part[4][TOP_F:], -2)
    near = [along_z(part[1], 1), along_z(part[-1], -1)]
    up2, down2 = call(relay_kernel, (shape((PIECE_F, K), F32),) * 2, size=2 << 20, n_in=6)(
        part[2], part[-2], up3, down3, up4, down4
    )
    far = [along_z(up2, 2), along_z(down2, -2)]
    return [part[0], *near, *far]


def step_tiles(step, ids, picked, columns, counts):
    part = {}
    got, grads = tiles(step, [0], ids, picked, [columns[0]], counts, None)
    part.update(got)
    near = [1, -1, 2, -2]
    got, grads = tiles(step, near, ids, picked, [columns[d] for d in near], counts, grads)
    part.update(got)
    far = [3, -3, 4]
    got, grads = tiles(
        step, far, ids, picked, [columns[3], columns[-3], *columns[4]], counts, grads, split=True
    )
    part.update(got)
    return part, grads


def column_update_kernel(grad_a, grad_b, block_ref, sums_ref, block_out, sums_out):
    grad = grad_a[:PIECE] + grad_b[:PIECE]
    new_sums = sums_ref[:PIECE] + grad * grad
    sums_out[:PIECE] = new_sums
    block_out[:PIECE] = (
        block_ref[:PIECE].astype(F32) - LEARN_RATE * grad * lax.rsqrt(new_sums)
    ).astype(BF16)
    bias_grad = (grad_a[PIECE:] + grad_b[PIECE:])[:1]
    bias_sums = sums_ref[PIECE:][:1] + bias_grad * bias_grad
    bias = block_ref[PIECE:].astype(F32)[:1] - LEARN_RATE * bias_grad * lax.rsqrt(bias_sums)
    row = lax.broadcasted_iota(jnp.int32, (8, K), 0)
    sums_out[PIECE:] = jnp.where(row == 0, bias_sums, 0.0)
    row = lax.broadcasted_iota(jnp.int32, (16, K), 0)
    block_out[PIECE:] = jnp.where(row == 0, bias, 0.0).astype(BF16)


def last_update_kernel(
    y_ref, grad_a, grad_b, block_ref, sums_ref, block_out, bias_out, sums_out, bias_sums_out
):
    y = y_ref[0]
    mine = pl.multiple_of(y * SHARD, SHARD)
    grad = grad_a[:SHARD] + grad_b[:SHARD]
    new_sums = sums_ref[pl.ds(mine, SHARD)] + grad * grad
    sums_out[...] = new_sums
    block_out[...] = (
        block_ref[pl.ds(mine, SHARD)].astype(F32) - LEARN_RATE * grad * lax.rsqrt(new_sums)
    ).astype(BF16)
    bias_grad = (grad_a[SHARD:] + grad_b[SHARD:])[:1, :SHARD]
    sums_tail = sums_ref[PIECE:][:1]
    bias_tail = block_ref[PIECE:].astype(F32)[:1]
    bias_sums = jnp.where(y == 0, sums_tail[:, :SHARD], sums_tail[:, SHARD:])
    bias = jnp.where(y == 0, bias_tail[:, :SHARD], bias_tail[:, SHARD:])
    bias_sums = bias_sums + bias_grad * bias_grad
    bias_sums_out[...] = bias_sums
    bias_out[...] = (bias - LEARN_RATE * bias_grad * lax.rsqrt(bias_sums)).astype(BF16)


def shards(
    row_factors,
    row_bias,
    row_sums,
    row_bias_sums,
    col_factors,
    col_bias,
    col_sums,
    col_bias_sums,
    row_pick,
    counts,
):
    at = lax.axis_index("group")
    y = (at % NY).astype(jnp.int32).reshape(1)
    ids = ((at // NY + jnp.arange(NZ)) % NZ).astype(jnp.int32)

    own_shard = pack(col_factors, col_bias)
    own = merge(y, own_shard, swap_y(own_shard))
    columns = gather_columns(own)

    pick_row = row_pick[0, 0]
    pick_col = pick_row.T
    table, bias, sums, bias_sums = (
        row_factors,
        row_bias.reshape(1, RTAB),
        row_sums,
        row_bias_sums.reshape(1, RTAB),
    )
    picked = gather(table, bias, pick_col)

    part, grads = step_tiles(0, ids, picked, columns, counts)
    total = sum(reduce_columns(part))
    table, bias, sums, bias_sums, *picked = row_update(
        0, False, *grads, table, bias, sums, bias_sums, pick_col, pick_row
    )

    shard_sums = pack(col_sums, col_bias_sums)
    held_block = next_stratum(own)
    held_sums = merge(y, next_stratum(shard_sums), next_stratum_swap_y(shard_sums))
    own, block_sums = call(
        column_update_kernel,
        (shape((PIECE_B, K), BF16), shape((PIECE_F, K), F32)),
        size=2 << 20,
        n_in=4,
    )(next_stratum(total), next_stratum_swap_y(total), held_block, held_sums)

    columns = gather_columns(own)
    part, grads = step_tiles(1, ids, picked, columns, counts)
    mine, theirs = call(
        split_sum_kernel,
        (shape((SHARD_F, K), F32),) * 2,
        size=2 << 20,
        specs=[SMEM] + [VMEM] * 5,
    )(y, *reduce_columns(part))
    table, bias, sums, bias_sums = row_update(
        1, True, *grads, table, bias, sums, bias_sums, pick_col, pick_row
    )
    held_block, held_sums = next_stratum(own), next_stratum(block_sums)
    new_block, new_bias, new_sums, new_bias_sums = call(
        last_update_kernel,
        (
            shape((SHARD, K), BF16),
            shape((1, SHARD), BF16),
            shape((SHARD, K), F32),
            shape((1, SHARD), F32),
        ),
        size=1 << 20,
        specs=[SMEM] + [VMEM] * 4,
    )(y, next_stratum(mine), next_stratum_swap_y(theirs), held_block, held_sums)
    return (
        table,
        bias.reshape(RTAB),
        sums,
        bias_sums.reshape(RTAB),
        new_block,
        new_bias.reshape(SHARD),
        new_sums,
        new_bias_sums.reshape(SHARD),
    )


def solution(mesh):
    both = P(("stratum", "group"))
    rows = P(("stratum", "group"), None)
    in_specs = (
        rows,
        both,
        rows,
        both,
        rows,
        both,
        rows,
        both,
        P("stratum", "group", None, None),
        P("stratum", "group", None, None, None),
    )
    out_specs = (rows, both, rows, both, rows, both, rows, both)
    return jax.shard_map(shards, mesh=mesh, in_specs=in_specs, out_specs=out_specs, check_vma=False)
```

```python
import functools

import jax
import jax.numpy as jnp
from jax import lax
from jax.experimental import pallas as pl
from jax.experimental.pallas import tpu as pltpu
from jax.sharding import PartitionSpec as P

LEARN_RATE = 0.2
COUNT_CAP = 100.0
POWER = 0.75

K = 256
BATCH = 512
RTAB = 1024
SHARD = 128
PIECE = 256
PIECE_B = PIECE + 16
PIECE_F = PIECE + 8
SHARD_B = SHARD + 16
SHARD_F = SHARD + 8
TOP = 144
NZ = 8
NY = 2

F32 = jnp.float32
BF16 = jnp.bfloat16
VMEM = pl.BlockSpec(memory_space=pltpu.VMEM)
SMEM = pl.BlockSpec(memory_space=pltpu.SMEM)


ANY = pl.BlockSpec(memory_space=pl.ANY)


def call(kernel, out_shape, flops=0, size=0, specs=None, n_in=0, n_after=0):
    specs = specs or [VMEM] * n_in
    n_read = len(specs)

    def body(*refs):
        kernel(*refs[:n_read], *refs[n_read + n_after :])

    return pl.pallas_call(
        body,
        out_shape=out_shape,
        in_specs=specs + [ANY] * n_after,
        out_specs=jax.tree.map(lambda _: VMEM, out_shape),
        cost_estimate=pl.CostEstimate(flops=flops, bytes_accessed=size, transcendentals=0),
        compiler_params=pltpu.CompilerParams(vmem_limit_bytes=32 * 1024 * 1024),
    )


def shape(dims, dtype):
    return jax.ShapeDtypeStruct(dims, dtype)


def along_z(block, distance):
    route = [(g, ((g // NY + distance) % NZ) * NY + g % NY) for g in range(NZ * NY)]
    return lax.ppermute(block, "group", route)


def swap_y(block):
    return lax.ppermute(block, "group", [(g, g ^ 1) for g in range(NZ * NY)])


def next_stratum(block):
    size = lax.axis_size("stratum")
    return lax.ppermute(block, "stratum", [(s, (s + 1) % size) for s in range(size)])


def next_stratum_swap_y(block):
    size = lax.axis_size("stratum")
    group = NZ * NY
    route = [
        (s * group + g, ((s + 1) % size) * group + (g ^ 1)) for s in range(size) for g in range(group)
    ]
    return lax.ppermute(block, ("stratum", "group"), route)


GRAIN = 700.0
REACH = 32760.0


def scale_code(top):
    return jnp.floor(jnp.log(jnp.maximum(top, 1e-18)) * GRAIN) + 2.0


def nearest(values):
    return jnp.clip(jnp.floor(values + 0.5), -32767.0, 32767.0).astype(jnp.int32).astype(jnp.int16)


def encode(grad, bias_grad):
    code = scale_code(jnp.max(jnp.abs(grad), axis=1, keepdims=True))
    data = nearest(grad * (jnp.exp(code * (-1.0 / GRAIN)) * REACH))
    codes = jnp.broadcast_to(code, (PIECE, 128)).T[:1]
    bias_code = scale_code(jnp.max(jnp.abs(bias_grad), axis=1, keepdims=True))
    scaled = bias_grad * (jnp.exp(bias_code * (-1.0 / GRAIN)) * REACH)
    high = jnp.floor(scaled + 0.5)
    low = (scaled - high) * REACH
    row = lax.broadcasted_iota(jnp.int32, (16, K), 0)
    tail = jnp.where(row == 0, high, jnp.where(row == 1, low, jnp.where(row == 2, bias_code, codes)))
    return data, nearest(tail)


def decode_rows(data, codes):
    scale = jnp.exp(codes * (1.0 / GRAIN)) * (1.0 / REACH)
    scale = jnp.broadcast_to(scale, (128, codes.shape[1])).T
    return data.astype(jnp.int32).astype(F32) * jnp.concatenate([scale, scale], axis=1)


def wide(tail):
    return tail.astype(jnp.int32).astype(F32)


def decode_bias(tail):
    scale = jnp.exp(tail[2:3] * (1.0 / GRAIN)) * (1.0 / REACH)
    return (tail[0:1] + tail[1:2] * (1.0 / REACH)) * scale


def decode(ref):
    tail = wide(ref[PIECE:])
    return decode_rows(ref[:PIECE], tail[3:4]), decode_bias(tail)


CODED = jax.ShapeDtypeStruct((PIECE_B, K), jnp.int16)
CODED_HALF = jax.ShapeDtypeStruct((SHARD_B, K), jnp.int16)


def store_coded(grad, bias_grad, *out_refs):
    data, tail = encode(grad, bias_grad)
    if len(out_refs) == 1:
        out_refs[0][:PIECE] = data
        out_refs[0][PIECE:] = tail
    else:
        for i, ref in enumerate(out_refs):
            ref[:SHARD] = data[i * SHARD : (i + 1) * SHARD]
            ref[SHARD:] = tail


def pack_kernel(rows_ref, bias_ref, out_ref):
    out_ref[:SHARD] = rows_ref[...]
    pad = out_ref.shape[0] - SHARD
    out_ref[SHARD:] = jnp.zeros((pad, K), out_ref.dtype)
    wide = jnp.concatenate([bias_ref[...], bias_ref[...]], axis=1).astype(F32)
    row = lax.broadcasted_iota(jnp.int32, (pad, K), 0)
    out_ref[SHARD:] = jnp.where(row == 0, jnp.broadcast_to(wide, (pad, K)), 0.0).astype(out_ref.dtype)


def pack(rows, bias):
    pad = 16 if rows.dtype == BF16 else 8
    return call(pack_kernel, shape((SHARD + pad, K), rows.dtype), n_in=2)(rows, bias.reshape(1, SHARD))


def merge_kernel(y_ref, own_ref, other_ref, out_ref):
    y = y_ref[0]
    mine = pl.multiple_of(y * SHARD, SHARD)
    theirs = pl.multiple_of((1 - y) * SHARD, SHARD)
    out_ref[pl.ds(mine, SHARD)] = own_ref[:SHARD]
    out_ref[pl.ds(theirs, SHARD)] = other_ref[:SHARD]
    a = own_ref[SHARD:].astype(F32)
    b = other_ref[SHARD:].astype(F32)
    lane = lax.broadcasted_iota(jnp.int32, a.shape, 1)
    out_ref[PIECE:] = jnp.where((lane < SHARD) == (y == 0), a, b).astype(out_ref.dtype)


def merge(y, own, other):
    pad = own.shape[0] - SHARD
    return call(
        merge_kernel, shape((PIECE + pad, K), own.dtype), specs=[SMEM, VMEM, VMEM]
    )(y, own, other)


def pick_rows(table, bias, pick_col, picked_ref, picked_bias_ref):
    lane = lax.broadcasted_iota(jnp.int32, (BATCH, RTAB), 1)
    hot = lane == pick_col
    one_hot = jnp.where(hot, 1.0, 0.0).astype(BF16)
    picked_ref[...] = jnp.dot(one_hot, table, preferred_element_type=F32).astype(BF16)
    column = jnp.sum(jnp.where(hot, bias, 0.0), axis=1, keepdims=True)
    picked_bias_ref[...] = jnp.broadcast_to(column, (BATCH, 128))


def gather_kernel(table_ref, bias_ref, pick_col_ref, picked_ref, picked_bias_ref):
    pick_rows(
        table_ref[...], bias_ref[...].astype(F32), pick_col_ref[:, :1], picked_ref, picked_bias_ref
    )


PICKED = (shape((BATCH, K), BF16), shape((BATCH, 128), F32))


def gather(table, bias, pick_col):
    return call(gather_kernel, PICKED, flops=2 * BATCH * RTAB * K, size=1 << 20, n_in=3)(
        table, bias, pick_col
    )


def row_update_kernel(
    step,
    grad_refs,
    bias_grad_refs,
    table_ref,
    bias_ref,
    sums_ref,
    bias_sums_ref,
    pick_col_ref,
    pick_row_ref,
    table_out,
    bias_out,
    sums_out,
    bias_sums_out,
    *picked_refs,
):
    grad = grad_refs[...]
    high = grad.astype(BF16)
    rest = grad - high.astype(F32)
    middle = rest.astype(BF16)
    low = (rest - middle.astype(F32)).astype(BF16)
    parts = jnp.concatenate([high, middle, low], axis=1)
    chunk = 256
    for c in range(RTAB // chunk):
        rows = slice(c * chunk, (c + 1) * chunk)
        index = lax.broadcasted_iota(jnp.int32, (chunk, BATCH), 0) + c * chunk
        spread = jnp.where(index == pick_row_ref[step : step + 1, :], 1.0, 0.0).astype(BF16)
        moved = jnp.dot(spread, parts, preferred_element_type=F32)
        full = moved[:, :K] + moved[:, K : 2 * K] + moved[:, 2 * K :]
        new_sums = sums_ref[rows] + full * full
        sums_out[rows] = new_sums
        table_out[rows] = (
            table_ref[rows].astype(F32) - LEARN_RATE * full * lax.rsqrt(new_sums)
        ).astype(BF16)
    column = jnp.sum(bias_grad_refs[...], axis=1, keepdims=True)
    lane = lax.broadcasted_iota(jnp.int32, (BATCH, RTAB), 1)
    hot = lane == pick_col_ref[:, step : step + 1]
    bias_grad = jnp.sum(jnp.where(hot, column, 0.0), axis=0, keepdims=True)
    new_bias_sums = bias_sums_ref[...] + bias_grad * bias_grad
    bias_sums_out[...] = new_bias_sums
    new_bias = (
        bias_ref[...].astype(F32) - LEARN_RATE * bias_grad * lax.rsqrt(new_bias_sums)
    ).astype(BF16)
    bias_out[...] = new_bias
    if picked_refs:
        pick_rows(
            table_out[...], new_bias.astype(F32), pick_col_ref[:, step + 1 : step + 2], *picked_refs
        )


def row_update(step, last, grad, bias_grad, table, bias, sums, bias_sums, pick_col, pick_row):
    outs = (
        shape((RTAB, K), BF16),
        shape((1, RTAB), BF16),
        shape((RTAB, K), F32),
        shape((1, RTAB), F32),
    )
    if not last:
        outs = outs + PICKED
    return call(
        functools.partial(row_update_kernel, step),
        outs,
        flops=8 * BATCH * RTAB * K,
        size=5 << 20,
        n_in=8,
    )(grad, bias_grad, table, bias, sums, bias_sums, pick_col, pick_row)


def tile_kernel(offsets, first, n_after, *refs):
    refs = list(refs)
    n, split = len(offsets), 4 in offsets
    refs.pop(0)
    picked_ref, picked_bias_ref = refs.pop(0), refs.pop(0)
    columns = [refs.pop(0) for _ in range(n + (1 if split else 0))]
    counts = [refs.pop(0) for _ in range(n)]
    if not first:
        grad_in, bias_in = refs.pop(0), refs.pop(0)
    refs = refs[n_after:]
    grad_out, bias_out = refs.pop(0), refs.pop(0)
    picked = picked_ref[...]
    picked_bias = jnp.concatenate([picked_bias_ref[...]] * 2, axis=1)
    row_grad = None if first else grad_in[...]
    row_bias_grad = None if first else bias_in[...]
    for i in range(n):
        if split and i == n - 1:
            top, bottom = columns[n - 1], columns[n]
            block = jnp.concatenate([top[...], bottom[: PIECE - TOP]], axis=0)
            tail = bottom[PIECE - TOP :]
        else:
            block, tail = columns[i][:PIECE], columns[i][PIECE:]
        bias = tail.astype(F32)[:1]
        scores = lax.dot_general(
            picked, block, (((1,), (1,)), ((), ())), preferred_element_type=F32
        )
        scores = scores + picked_bias + bias
        counted = counts[i][...].astype(F32)
        target = jnp.log(jnp.maximum(counted, 1.0))
        weight = jnp.exp(POWER * target - POWER * jnp.log(jnp.float32(COUNT_CAP)))
        weight = jnp.where(counted > 0.0, jnp.minimum(weight, 1.0), 0.0)
        residual = weight * (scores - target)
        half = residual.astype(BF16)
        part = jnp.dot(half, block, preferred_element_type=F32)
        row_grad = part if row_grad is None else row_grad + part
        lanes = residual[:, :128] + residual[:, 128:]
        row_bias_grad = lanes if row_bias_grad is None else row_bias_grad + lanes
        col_grad = lax.dot_general(
            half, picked, (((0,), (0,)), ((), ())), preferred_element_type=F32
        )
        bias_grad = jnp.sum(residual, axis=0, keepdims=True)
        if offsets[i] in LOCAL:
            out = refs.pop(0)
            out[:PIECE] = col_grad
            out[PIECE:] = jnp.broadcast_to(bias_grad, (PIECE_F - PIECE, K))
        else:
            store_coded(col_grad, bias_grad, *[refs.pop(0) for _ in range(2 if offsets[i] == 4 else 1)])
    grad_out[...] = row_grad
    bias_out[...] = row_bias_grad


LOCAL = (0, 2, -2)


def tiles(step, offsets, ids, picked, columns, counts, grads, after=()):
    n = len(offsets)
    first = grads is None

    def whole(dims):
        return pl.BlockSpec(dims, lambda i, ids: (0, 0))

    specs = [whole((BATCH, K)), whole((BATCH, 128))]
    specs += [whole(c.shape) for c in columns]
    for offset in offsets:
        specs.append(
            pl.BlockSpec(
                (None, None, None, BATCH, PIECE),
                functools.partial(lambda at, i, ids: (0, 0, step, 0, ids[at]), offset % NZ),
            )
        )
    args = [*picked, *columns, *([counts] * n)]
    if not first:
        specs += [whole((BATCH, K)), whole((BATCH, 128))]
        args += list(grads)
    specs += [ANY] * len(after)
    args += list(after)
    out_shape = [shape((BATCH, K), F32), shape((BATCH, 128), F32)]
    for offset in offsets:
        if offset in LOCAL:
            out_shape.append(shape((PIECE_F, K), F32))
        else:
            out_shape += [CODED_HALF] * 2 if offset == 4 else [CODED]
    out_specs = [whole(o.shape) for o in out_shape]
    outs = pl.pallas_call(
        functools.partial(tile_kernel, offsets, first, len(after)),
        grid_spec=pltpu.PrefetchScalarGridSpec(
            num_scalar_prefetch=1, grid=(1,), in_specs=specs, out_specs=out_specs
        ),
        out_shape=out_shape,
        cost_estimate=pl.CostEstimate(
            flops=n * 6 * BATCH * PIECE * K,
            bytes_accessed=n * (BATCH * PIECE * 4 + PIECE * K * 6),
            transcendentals=2 * n * BATCH * PIECE,
        ),
        compiler_params=pltpu.CompilerParams(vmem_limit_bytes=40 * 1024 * 1024),
    )(ids, *args)
    part = {o: (outs[i + 2], outs[i + 3]) if o == 4 else outs[i + 2] for i, o in enumerate(offsets)}
    return part, tuple(outs[:2])


def relay_kernel(up_ref, down_ref, up3_ref, down3_ref, up4_ref, down4_ref, up_out, down_out):
    for ref, far_ref, half_ref, out, top in (
        (up_ref, up3_ref, up4_ref, up_out, True),
        (down_ref, down3_ref, down4_ref, down_out, False),
    ):
        grad, bias_grad = decode(far_ref)
        tail = wide(half_ref[SHARD:])
        codes = tail[3:4]
        mine = codes[:, :SHARD] if top else codes[:, SHARD:]
        half = decode_rows(half_ref[:SHARD], mine)
        zero = jnp.zeros_like(half)
        grad = grad + ref[:PIECE] + jnp.concatenate([half, zero] if top else [zero, half], axis=0)
        bias_grad = bias_grad + ref[PIECE:][:1]
        if top:
            bias_grad = bias_grad + decode_bias(tail)
        store_coded(grad, bias_grad, out)


def column_total(own_ref, refs):
    grad, bias_grad = own_ref[:PIECE], own_ref[PIECE:][:1]
    for ref in refs:
        more, more_bias = decode(ref)
        grad, bias_grad = grad + more, bias_grad + more_bias
    return grad, bias_grad


def sum_kernel(own_ref, a, b, c, d, out):
    store_coded(*column_total(own_ref, (a, b, c, d)), out)


def split_sum_kernel(y_ref, own_ref, a, b, c, d, mine_out, theirs_out, held):
    store_coded(*column_total(own_ref, (a, b, c, d)), held)
    y = y_ref[0]
    mine = pl.multiple_of(y * SHARD, SHARD)
    theirs = pl.multiple_of((1 - y) * SHARD, SHARD)
    mine_out[:SHARD] = held[pl.ds(mine, SHARD)]
    theirs_out[:SHARD] = held[pl.ds(theirs, SHARD)]
    mine_out[SHARD:] = held[PIECE:]
    theirs_out[SHARD:] = held[PIECE:]


def gather_columns(own):
    up1, down1 = along_z(own, -1), along_z(own, 1)
    up2, down2 = along_z(own, -2), along_z(own, 2)
    up3, down3 = along_z(up2, -1), along_z(down2, 1)
    top4, bottom4 = along_z(up2[:TOP], -2), along_z(down2[TOP:], 2)
    return {0: own, 1: up1, -1: down1, 2: up2, -2: down2, 3: up3, -3: down3, 4: (top4, bottom4)}


def reduce_columns(part, after):
    up3, down3 = along_z(part[3], 1), along_z(part[-3], -1)
    up4, down4 = along_z(part[4][0], 2), along_z(part[4][1], -2)
    near = [along_z(part[1], 1), along_z(part[-1], -1)]
    up2, down2 = call(relay_kernel, (CODED,) * 2, size=2 << 20, n_in=6, n_after=len(after))(
        part[2], part[-2], up3, down3, up4, down4, *after
    )
    return [part[0], *near, along_z(up2, 2), along_z(down2, -2)]


def step_tiles(step, ids, picked, columns, counts, after):
    part = {}
    got, grads = tiles(step, [0], ids, picked, [columns[0]], counts, None, after[0])
    part.update(got)
    near = [1, -1, 2, -2]
    got, grads = tiles(step, near, ids, picked, [columns[d] for d in near], counts, grads, after[1])
    part.update(got)
    far = [3, -3, 4]
    far_columns = [columns[3], columns[-3], *columns[4]]
    got, grads = tiles(step, far, ids, picked, far_columns, counts, grads, after[2])
    part.update(got)
    return part, grads


def column_update_kernel(a_ref, b_ref, block_ref, sums_ref, block_out, sums_out):
    grad, bias_grad = decode(a_ref)
    more, more_bias = decode(b_ref)
    grad, bias_grad = grad + more, bias_grad + more_bias
    new_sums = sums_ref[:PIECE] + grad * grad
    sums_out[:PIECE] = new_sums
    block_out[:PIECE] = (
        block_ref[:PIECE].astype(F32) - LEARN_RATE * grad * lax.rsqrt(new_sums)
    ).astype(BF16)
    bias_sums = sums_ref[PIECE:][:1] + bias_grad * bias_grad
    bias = block_ref[PIECE:].astype(F32)[:1] - LEARN_RATE * bias_grad * lax.rsqrt(bias_sums)
    row = lax.broadcasted_iota(jnp.int32, (8, K), 0)
    sums_out[PIECE:] = jnp.where(row == 0, bias_sums, 0.0)
    row = lax.broadcasted_iota(jnp.int32, (16, K), 0)
    block_out[PIECE:] = jnp.where(row == 0, bias, 0.0).astype(BF16)


def last_update_kernel(
    y_ref, a_ref, b_ref, block_ref, sums_ref, block_out, bias_out, sums_out, bias_sums_out
):
    y = y_ref[0]
    mine = pl.multiple_of(y * SHARD, SHARD)
    grad, bias_grad = 0.0, 0.0
    for ref in (a_ref, b_ref):
        tail = wide(ref[SHARD:])
        codes = jnp.where(y == 0, tail[3:4, :SHARD], tail[3:4, SHARD:])
        grad = grad + decode_rows(ref[:SHARD], codes)
        bias_grad = bias_grad + decode_bias(tail)
    bias_grad = jnp.where(y == 0, bias_grad[:, :SHARD], bias_grad[:, SHARD:])
    new_sums = sums_ref[pl.ds(mine, SHARD)] + grad * grad
    sums_out[...] = new_sums
    block_out[...] = (
        block_ref[pl.ds(mine, SHARD)].astype(F32) - LEARN_RATE * grad * lax.rsqrt(new_sums)
    ).astype(BF16)
    sums_tail = sums_ref[PIECE:][:1]
    bias_tail = block_ref[PIECE:].astype(F32)[:1]
    bias_sums = jnp.where(y == 0, sums_tail[:, :SHARD], sums_tail[:, SHARD:])
    bias = jnp.where(y == 0, bias_tail[:, :SHARD], bias_tail[:, SHARD:])
    bias_sums = bias_sums + bias_grad * bias_grad
    bias_sums_out[...] = bias_sums
    bias_out[...] = (bias - LEARN_RATE * bias_grad * lax.rsqrt(bias_sums)).astype(BF16)


def shards(
    row_factors,
    row_bias,
    row_sums,
    row_bias_sums,
    col_factors,
    col_bias,
    col_sums,
    col_bias_sums,
    row_pick,
    counts,
):
    at = lax.axis_index("group")
    y = (at % NY).astype(jnp.int32).reshape(1)
    ids = ((at // NY + jnp.arange(NZ)) % NZ).astype(jnp.int32)

    own_shard = pack(col_factors, col_bias)
    shard_sums = pack(col_sums, col_bias_sums)
    own = merge(y, own_shard, swap_y(own_shard))
    columns = gather_columns(own)
    held_sums = merge(y, next_stratum(shard_sums), next_stratum_swap_y(shard_sums))
    held_block = next_stratum(own)

    pick_row = row_pick[0, 0]
    pick_col = pick_row.T
    table, bias, sums, bias_sums = (
        row_factors,
        row_bias.reshape(1, RTAB),
        row_sums,
        row_bias_sums.reshape(1, RTAB),
    )
    picked = gather(table, bias, pick_col)

    after = ((held_sums,), (held_block,), ())
    part, grads = step_tiles(0, ids, picked, columns, counts, after)
    table, bias, sums, bias_sums, *picked = row_update(
        0, False, *grads, table, bias, sums, bias_sums, pick_col, pick_row
    )
    total = call(sum_kernel, CODED, size=1 << 20, n_in=5)(*reduce_columns(part, (picked[0],)))
    own, block_sums = call(
        column_update_kernel,
        (shape((PIECE_B, K), BF16), shape((PIECE_F, K), F32)),
        size=2 << 20,
        n_in=4,
    )(next_stratum(total), next_stratum_swap_y(total), held_block, held_sums)

    columns = gather_columns(own)
    held_block, held_sums = next_stratum(own), next_stratum(block_sums)
    after = ((), (held_block,), (held_sums,))
    part, grads = step_tiles(1, ids, picked, columns, counts, after)
    table, bias, sums, bias_sums = row_update(
        1, True, *grads, table, bias, sums, bias_sums, pick_col, pick_row
    )
    mine, theirs, _ = call(
        split_sum_kernel,
        (CODED_HALF, CODED_HALF, CODED),
        size=1 << 20,
        specs=[SMEM] + [VMEM] * 5,
    )(y, *reduce_columns(part, (bias,)))
    new_block, new_bias, new_sums, new_bias_sums = call(
        last_update_kernel,
        (
            shape((SHARD, K), BF16),
            shape((1, SHARD), BF16),
            shape((SHARD, K), F32),
            shape((1, SHARD), F32),
        ),
        size=1 << 20,
        specs=[SMEM] + [VMEM] * 4,
    )(y, next_stratum(mine), next_stratum_swap_y(theirs), held_block, held_sums)
    return (
        table,
        bias.reshape(RTAB),
        sums,
        bias_sums.reshape(RTAB),
        new_block,
        new_bias.reshape(SHARD),
        new_sums,
        new_bias_sums.reshape(SHARD),
    )


def solution(mesh):
    both = P(("stratum", "group"))
    rows = P(("stratum", "group"), None)
    in_specs = (
        rows,
        both,
        rows,
        both,
        rows,
        both,
        rows,
        both,
        P("stratum", "group", None, None),
        P("stratum", "group", None, None, None),
    )
    out_specs = (rows, both, rows, both, rows, both, rows, both)
    return jax.shard_map(shards, mesh=mesh, in_specs=in_specs, out_specs=out_specs, check_vma=False)
```

```python
import functools

import jax
import jax.numpy as jnp
from jax import lax
from jax.experimental import pallas as pl
from jax.experimental.pallas import tpu as pltpu
from jax.sharding import PartitionSpec as P

LEARN_RATE = 0.2
COUNT_CAP = 100.0
POWER = 0.75

K = 256
BATCH = 512
RTAB = 1024
SHARD = 128
PIECE = 256
PIECE_B = PIECE + 16
PIECE_F = PIECE + 8
SHARD_B = SHARD + 16
SHARD_F = SHARD + 8
NZ = 8
NY = 2

F32 = jnp.float32
BF16 = jnp.bfloat16
VMEM = pl.BlockSpec(memory_space=pltpu.VMEM)
SMEM = pl.BlockSpec(memory_space=pltpu.SMEM)


ANY = pl.BlockSpec(memory_space=pl.ANY)


def call(kernel, out_shape, flops=0, size=0, specs=None, n_in=0, n_after=0):
    specs = specs or [VMEM] * n_in
    n_read = len(specs)

    def body(*refs):
        kernel(*refs[:n_read], *refs[n_read + n_after :])

    return pl.pallas_call(
        body,
        out_shape=out_shape,
        in_specs=specs + [ANY] * n_after,
        out_specs=jax.tree.map(lambda _: VMEM, out_shape),
        cost_estimate=pl.CostEstimate(flops=0, bytes_accessed=0, transcendentals=0),
        compiler_params=pltpu.CompilerParams(vmem_limit_bytes=16 * 1024 * 1024),
    )


def shape(dims, dtype):
    return jax.ShapeDtypeStruct(dims, dtype)


def along_z(block, distance):
    route = [(g, ((g // NY + distance) % NZ) * NY + g % NY) for g in range(NZ * NY)]
    return lax.ppermute(block, "group", route)


def swap_y(block):
    return lax.ppermute(block, "group", [(g, g ^ 1) for g in range(NZ * NY)])


def next_stratum(block):
    size = lax.axis_size("stratum")
    return lax.ppermute(block, "stratum", [(s, (s + 1) % size) for s in range(size)])


def next_stratum_swap_y(block):
    size = lax.axis_size("stratum")
    group = NZ * NY
    route = [
        (s * group + g, ((s + 1) % size) * group + (g ^ 1)) for s in range(size) for g in range(group)
    ]
    return lax.ppermute(block, ("stratum", "group"), route)


GRAIN = 700.0
REACH = 32760.0


def scale_code(top):
    return jnp.floor(jnp.log(jnp.maximum(top, 1e-18)) * GRAIN) + 2.0


def nearest(values):
    return jnp.clip(jnp.floor(values + 0.5), -32767.0, 32767.0).astype(jnp.int32).astype(jnp.int16)


def encode(grad, bias_grad):
    code = scale_code(jnp.max(jnp.abs(grad), axis=1, keepdims=True))
    data = nearest(grad * (jnp.exp(code * (-1.0 / GRAIN)) * REACH))
    codes = jnp.broadcast_to(code, (PIECE, 128)).T[:1]
    bias_code = scale_code(jnp.max(jnp.abs(bias_grad), axis=1, keepdims=True))
    scaled = bias_grad * (jnp.exp(bias_code * (-1.0 / GRAIN)) * REACH)
    high = jnp.floor(scaled + 0.5)
    low = (scaled - high) * REACH
    row = lax.broadcasted_iota(jnp.int32, (16, K), 0)
    tail = jnp.where(row == 0, high, jnp.where(row == 1, low, jnp.where(row == 2, bias_code, codes)))
    return data, nearest(tail)


def decode_rows(data, codes):
    scale = jnp.exp(codes * (1.0 / GRAIN)) * (1.0 / REACH)
    scale = jnp.broadcast_to(scale, (128, codes.shape[1])).T
    return data.astype(jnp.int32).astype(F32) * jnp.concatenate([scale, scale], axis=1)


def wide(tail):
    return tail.astype(jnp.int32).astype(F32)


def decode_bias(tail):
    scale = jnp.exp(tail[2:3] * (1.0 / GRAIN)) * (1.0 / REACH)
    return (tail[0:1] + tail[1:2] * (1.0 / REACH)) * scale


def decode(ref):
    tail = wide(ref[PIECE:])
    return decode_rows(ref[:PIECE], tail[3:4]), decode_bias(tail)


CODED = jax.ShapeDtypeStruct((PIECE_B, K), jnp.int16)
CODED_HALF = jax.ShapeDtypeStruct((SHARD_B, K), jnp.int16)


def store_coded(grad, bias_grad, out_ref):
    data, tail = encode(grad, bias_grad)
    out_ref[:PIECE] = data
    out_ref[PIECE:] = tail


def pack_kernel(rows_ref, bias_ref, out_ref):
    out_ref[:SHARD] = rows_ref[...]
    pad = out_ref.shape[0] - SHARD
    out_ref[SHARD:] = jnp.zeros((pad, K), out_ref.dtype)
    wide = jnp.concatenate([bias_ref[...], bias_ref[...]], axis=1).astype(F32)
    row = lax.broadcasted_iota(jnp.int32, (pad, K), 0)
    out_ref[SHARD:] = jnp.where(row == 0, jnp.broadcast_to(wide, (pad, K)), 0.0).astype(out_ref.dtype)


def pack(rows, bias):
    pad = 16 if rows.dtype == BF16 else 8
    return call(pack_kernel, shape((SHARD + pad, K), rows.dtype), n_in=2)(rows, bias.reshape(1, SHARD))


def merge_kernel(y_ref, own_ref, other_ref, out_ref):
    y = y_ref[0]
    mine = pl.multiple_of(y * SHARD, SHARD)
    theirs = pl.multiple_of((1 - y) * SHARD, SHARD)
    out_ref[pl.ds(mine, SHARD)] = own_ref[:SHARD]
    out_ref[pl.ds(theirs, SHARD)] = other_ref[:SHARD]
    a = own_ref[SHARD:].astype(F32)
    b = other_ref[SHARD:].astype(F32)
    lane = lax.broadcasted_iota(jnp.int32, a.shape, 1)
    out_ref[PIECE:] = jnp.where((lane < SHARD) == (y == 0), a, b).astype(out_ref.dtype)


def merge(y, own, other, after):
    return call(
        merge_kernel, shape((PIECE_B, K), BF16), specs=[SMEM, VMEM, VMEM], n_after=len(after)
    )(y, own, other, *after)


HELD = jax.ShapeDtypeStruct((SHARD_F, 2 * K), F32)


def hold_kernel(block_ref, bias_ref, sums_ref, bias_sums_ref, out_ref):
    out_ref[:SHARD, :K] = block_ref[...].astype(F32)
    out_ref[:SHARD, K:] = sums_ref[...]
    both = [bias_ref[...].astype(F32)] * 2 + [bias_sums_ref[...]] * 2
    out_ref[SHARD:] = jnp.broadcast_to(jnp.concatenate(both, axis=1), (8, 2 * K))


def hold_half_kernel(y_ref, block_ref, sums_ref, out_ref):
    y = y_ref[0]
    mine = pl.multiple_of(y * SHARD, SHARD)
    out_ref[:SHARD, :K] = block_ref[pl.ds(mine, SHARD)].astype(F32)
    out_ref[:SHARD, K:] = sums_ref[pl.ds(mine, SHARD)]
    both = []
    for tail in (block_ref[PIECE:].astype(F32)[:1], sums_ref[PIECE:][:1]):
        both += [jnp.where(y == 0, tail[:, :SHARD], tail[:, SHARD:])] * 2
    out_ref[SHARD:] = jnp.broadcast_to(jnp.concatenate(both, axis=1), (8, 2 * K))


def pick_rows(table, bias, pick_col, picked_ref, picked_bias_ref):
    lane = lax.broadcasted_iota(jnp.int32, (BATCH, RTAB), 1)
    hot = lane == pick_col
    one_hot = jnp.where(hot, 1.0, 0.0).astype(BF16)
    picked_ref[...] = jnp.dot(one_hot, table, preferred_element_type=F32).astype(BF16)
    column = jnp.sum(jnp.where(hot, bias, 0.0), axis=1, keepdims=True)
    picked_bias_ref[...] = jnp.broadcast_to(column, (BATCH, 128))


def gather_kernel(table_ref, bias_ref, pick_col_ref, picked_ref, picked_bias_ref):
    pick_rows(
        table_ref[...], bias_ref[...].astype(F32), pick_col_ref[:, :1], picked_ref, picked_bias_ref
    )


PICKED = (shape((BATCH, K), BF16), shape((BATCH, 128), F32))


def gather(table, bias, pick_col):
    return call(gather_kernel, PICKED, n_in=3)(
        table, bias, pick_col
    )


def row_update_kernel(
    step,
    grad_refs,
    bias_grad_refs,
    table_ref,
    bias_ref,
    sums_ref,
    bias_sums_ref,
    pick_col_ref,
    pick_row_ref,
    table_out,
    bias_out,
    sums_out,
    bias_sums_out,
    *picked_refs,
):
    grad = grad_refs[...]
    high = grad.astype(BF16)
    rest = grad - high.astype(F32)
    middle = rest.astype(BF16)
    low = (rest - middle.astype(F32)).astype(BF16)
    parts = jnp.concatenate([high, middle, low], axis=1)
    chunk = 256
    for c in range(RTAB // chunk):
        rows = slice(c * chunk, (c + 1) * chunk)
        index = lax.broadcasted_iota(jnp.int32, (chunk, BATCH), 0) + c * chunk
        spread = jnp.where(index == pick_row_ref[step : step + 1, :], 1.0, 0.0).astype(BF16)
        moved = jnp.dot(spread, parts, preferred_element_type=F32)
        full = moved[:, :K] + moved[:, K : 2 * K] + moved[:, 2 * K :]
        new_sums = sums_ref[rows] + full * full
        sums_out[rows] = new_sums
        table_out[rows] = (
            table_ref[rows].astype(F32) - LEARN_RATE * full * lax.rsqrt(new_sums)
        ).astype(BF16)
    column = jnp.sum(bias_grad_refs[...], axis=1, keepdims=True)
    lane = lax.broadcasted_iota(jnp.int32, (BATCH, RTAB), 1)
    hot = lane == pick_col_ref[:, step : step + 1]
    bias_grad = jnp.sum(jnp.where(hot, column, 0.0), axis=0, keepdims=True)
    new_bias_sums = bias_sums_ref[...] + bias_grad * bias_grad
    bias_sums_out[...] = new_bias_sums
    new_bias = (
        bias_ref[...].astype(F32) - LEARN_RATE * bias_grad * lax.rsqrt(new_bias_sums)
    ).astype(BF16)
    bias_out[...] = new_bias
    if picked_refs:
        pick_rows(
            table_out[...], new_bias.astype(F32), pick_col_ref[:, step + 1 : step + 2], *picked_refs
        )


def row_update(step, last, grad, bias_grad, table, bias, sums, bias_sums, pick_col, pick_row):
    outs = (
        shape((RTAB, K), BF16),
        shape((1, RTAB), BF16),
        shape((RTAB, K), F32),
        shape((1, RTAB), F32),
    )
    if not last:
        outs = outs + PICKED
    return call(
        functools.partial(row_update_kernel, step),
        outs,
        flops=8 * BATCH * RTAB * K,
        size=5 << 20,
        n_in=8,
    )(grad, bias_grad, table, bias, sums, bias_sums, pick_col, pick_row)


def tile_kernel(offsets, first, n_after, *refs):
    refs = list(refs)
    n = len(offsets)
    refs.pop(0)
    picked_ref, picked_bias_ref = refs.pop(0), refs.pop(0)
    columns = [refs.pop(0) for _ in range(n)]
    counts = [refs.pop(0) for _ in range(n)]
    if not first:
        grad_in, bias_in = refs.pop(0), refs.pop(0)
    refs = refs[n_after:]
    grad_out, bias_out = refs.pop(0), refs.pop(0)
    picked = picked_ref[...]
    picked_bias = jnp.concatenate([picked_bias_ref[...]] * 2, axis=1)
    row_grad = None if first else grad_in[...]
    row_bias_grad = None if first else bias_in[...]
    for i in range(n):
        block, tail = columns[i][:PIECE], columns[i][PIECE:]
        bias = tail.astype(F32)[:1]
        scores = lax.dot_general(
            picked, block, (((1,), (1,)), ((), ())), preferred_element_type=F32
        )
        scores = scores + picked_bias + bias
        counted = counts[i][...].astype(F32)
        target = jnp.log(jnp.maximum(counted, 1.0))
        weight = jnp.exp(POWER * target - POWER * jnp.log(jnp.float32(COUNT_CAP)))
        weight = jnp.where(counted > 0.0, jnp.minimum(weight, 1.0), 0.0)
        residual = weight * (scores - target)
        half = residual.astype(BF16)
        part = jnp.dot(half, block, preferred_element_type=F32)
        row_grad = part if row_grad is None else row_grad + part
        lanes = residual[:, :128] + residual[:, 128:]
        row_bias_grad = lanes if row_bias_grad is None else row_bias_grad + lanes
        col_grad = lax.dot_general(
            half, picked, (((0,), (0,)), ((), ())), preferred_element_type=F32
        )
        bias_grad = jnp.sum(residual, axis=0, keepdims=True)
        if offsets[i] in LOCAL:
            out = refs.pop(0)
            out[:PIECE] = col_grad
            out[PIECE:] = jnp.broadcast_to(bias_grad, (PIECE_F - PIECE, K))
        else:
            store_coded(col_grad, bias_grad, refs.pop(0))
    grad_out[...] = row_grad
    bias_out[...] = row_bias_grad


LOCAL = (0, 2, -2)


def tiles(step, offsets, ids, picked, columns, counts, grads, after=()):
    n = len(offsets)
    first = grads is None

    def whole(dims):
        return pl.BlockSpec(dims, lambda i, ids: (0, 0))

    specs = [whole((BATCH, K)), whole((BATCH, 128))]
    specs += [whole(c.shape) for c in columns]
    for offset in offsets:
        specs.append(
            pl.BlockSpec(
                (None, None, None, BATCH, PIECE),
                functools.partial(lambda at, i, ids: (0, 0, step, 0, ids[at]), offset % NZ),
            )
        )
    args = [*picked, *columns, *([counts] * n)]
    if not first:
        specs += [whole((BATCH, K)), whole((BATCH, 128))]
        args += list(grads)
    specs += [ANY] * len(after)
    args += list(after)
    out_shape = [shape((BATCH, K), F32), shape((BATCH, 128), F32)]
    for offset in offsets:
        if offset in LOCAL:
            out_shape.append(shape((PIECE_F, K), F32))
        else:
            out_shape.append(CODED)
    out_specs = [whole(o.shape) for o in out_shape]
    outs = pl.pallas_call(
        functools.partial(tile_kernel, offsets, first, len(after)),
        grid_spec=pltpu.PrefetchScalarGridSpec(
            num_scalar_prefetch=1, grid=(1,), in_specs=specs, out_specs=out_specs
        ),
        out_shape=out_shape,
        cost_estimate=pl.CostEstimate(flops=0, bytes_accessed=0, transcendentals=0),
        compiler_params=pltpu.CompilerParams(vmem_limit_bytes=24 * 1024 * 1024),
    )(ids, *args)
    return dict(zip(offsets, outs[2:])), tuple(outs[:2])


def relay_kernel(up_ref, down_ref, up3_ref, down3_ref, up4_ref, up_out, down_out):
    store_coded(*column_total(up_ref, (up3_ref, up4_ref)), up_out)
    store_coded(*column_total(down_ref, (down3_ref,)), down_out)


def column_total(own_ref, refs):
    grad, bias_grad = own_ref[:PIECE], own_ref[PIECE:][:1]
    for ref in refs:
        more, more_bias = decode(ref)
        grad, bias_grad = grad + more, bias_grad + more_bias
    return grad, bias_grad


def sum_kernel(own_ref, a, b, c, d, out):
    store_coded(*column_total(own_ref, (a, b, c, d)), out)


def split_sum_kernel(y_ref, own_ref, a, b, c, d, mine_out, theirs_out, held):
    store_coded(*column_total(own_ref, (a, b, c, d)), held)
    y = y_ref[0]
    mine = pl.multiple_of(y * SHARD, SHARD)
    theirs = pl.multiple_of((1 - y) * SHARD, SHARD)
    mine_out[:SHARD] = held[pl.ds(mine, SHARD)]
    theirs_out[:SHARD] = held[pl.ds(theirs, SHARD)]
    mine_out[SHARD:] = held[PIECE:]
    theirs_out[SHARD:] = held[PIECE:]


def gather_columns(own):
    up1, down1 = along_z(own, -1), along_z(own, 1)
    up2, down2 = along_z(own, -2), along_z(own, 2)
    up3, down3 = along_z(up2, -1), along_z(down2, 1)
    far = along_z(up2, -2)
    return {0: own, 1: up1, -1: down1, 2: up2, -2: down2, 3: up3, -3: down3, 4: far}


def reduce_columns(part, after):
    up3, down3 = along_z(part[3], 1), along_z(part[-3], -1)
    up4 = along_z(part[4], 2)
    near = [along_z(part[1], 1), along_z(part[-1], -1)]
    up2, down2 = call(relay_kernel, (CODED,) * 2, size=2 << 20, n_in=5, n_after=len(after))(
        part[2], part[-2], up3, down3, up4, *after
    )
    return [part[0], *near, along_z(up2, 2), along_z(down2, -2)]


def step_tiles(step, ids, picked, columns, counts):
    part = {}
    got, grads = tiles(step, [0], ids, picked, [columns[0]], counts, None)
    part.update(got)
    near = [1, -1, 2, -2]
    got, grads = tiles(step, near, ids, picked, [columns[d] for d in near], counts, grads)
    part.update(got)
    near_grad = grads[1]
    far = [3, -3, 4]
    far_columns = [columns[3], columns[-3], columns[4]]
    got, grads = tiles(step, far, ids, picked, far_columns, counts, grads)
    part.update(got)
    return part, grads, near_grad


def column_update_kernel(y_ref, a_ref, b_ref, held_a, held_b, block_out, sums_out):
    y = y_ref[0]
    grad, bias_grad = decode(a_ref)
    more, more_bias = decode(b_ref)
    grad, bias_grad = grad + more, bias_grad + more_bias
    tails = [held_a[SHARD:][:1], held_b[SHARD:][:1]]
    for half in range(2):
        rows = slice(half * SHARD, (half + 1) * SHARD)
        held = jnp.where(y == half, held_a[:SHARD], held_b[:SHARD])
        new_sums = held[:, K:] + grad[rows] * grad[rows]
        sums_out[rows] = new_sums
        block_out[rows] = (
            held[:, :K] - LEARN_RATE * grad[rows] * lax.rsqrt(new_sums)
        ).astype(BF16)
    lane = lax.broadcasted_iota(jnp.int32, (1, 2 * K), 1) % K
    tail = jnp.where((lane < SHARD) == (y == 0), tails[0], tails[1])
    bias_sums = tail[:, K:] + bias_grad * bias_grad
    bias = tail[:, :K] - LEARN_RATE * bias_grad * lax.rsqrt(bias_sums)
    row = lax.broadcasted_iota(jnp.int32, (8, K), 0)
    sums_out[PIECE:] = jnp.where(row == 0, bias_sums, 0.0)
    row = lax.broadcasted_iota(jnp.int32, (16, K), 0)
    block_out[PIECE:] = jnp.where(row == 0, bias, 0.0).astype(BF16)


def last_update_kernel(
    y_ref, a_ref, b_ref, held_ref, block_out, bias_out, sums_out, bias_sums_out
):
    y = y_ref[0]
    grad, bias_grad = 0.0, 0.0
    for ref in (a_ref, b_ref):
        tail = wide(ref[SHARD:])
        codes = jnp.where(y == 0, tail[3:4, :SHARD], tail[3:4, SHARD:])
        grad = grad + decode_rows(ref[:SHARD], codes)
        bias_grad = bias_grad + decode_bias(tail)
    bias_grad = jnp.where(y == 0, bias_grad[:, :SHARD], bias_grad[:, SHARD:])
    new_sums = held_ref[:SHARD, K:] + grad * grad
    sums_out[...] = new_sums
    block_out[...] = (
        held_ref[:SHARD, :K] - LEARN_RATE * grad * lax.rsqrt(new_sums)
    ).astype(BF16)
    tail = held_ref[SHARD:][:1]
    bias_sums = tail[:, K : K + SHARD] + bias_grad * bias_grad
    bias_sums_out[...] = bias_sums
    bias_out[...] = (tail[:, :SHARD] - LEARN_RATE * bias_grad * lax.rsqrt(bias_sums)).astype(BF16)


def shards(
    row_factors,
    row_bias,
    row_sums,
    row_bias_sums,
    col_factors,
    col_bias,
    col_sums,
    col_bias_sums,
    row_pick,
    counts,
):
    at = lax.axis_index("group")
    y = (at % NY).astype(jnp.int32).reshape(1)
    ids = ((at // NY + jnp.arange(NZ)) % NZ).astype(jnp.int32)

    own_shard = pack(col_factors, col_bias)
    other_shard = swap_y(own_shard)
    pick_row = row_pick[0, 0]
    pick_col = pick_row.T
    table, bias, sums, bias_sums = (
        row_factors,
        row_bias.reshape(1, RTAB),
        row_sums,
        row_bias_sums.reshape(1, RTAB),
    )
    picked = gather(table, bias, pick_col)
    own = merge(y, own_shard, other_shard, (picked[0],))
    columns = gather_columns(own)

    part, grads, near_grad = step_tiles(0, ids, picked, columns, counts)
    held = call(hold_kernel, HELD, n_in=4, n_after=1)(
        col_factors, col_bias.reshape(1, SHARD), col_sums, col_bias_sums.reshape(1, SHARD), near_grad
    )
    held = (next_stratum(held), next_stratum_swap_y(held))
    table, bias, sums, bias_sums, *picked = row_update(
        0, False, *grads, table, bias, sums, bias_sums, pick_col, pick_row
    )
    total = call(sum_kernel, CODED, size=1 << 20, n_in=5)(*reduce_columns(part, (picked[0], *held)))
    own, block_sums = call(
        column_update_kernel,
        (shape((PIECE_B, K), BF16), shape((PIECE_F, K), F32)),
        size=2 << 20,
        specs=[SMEM] + [VMEM] * 4,
    )(y, next_stratum(total), next_stratum_swap_y(total), *held)

    columns = gather_columns(own)
    part, grads, near_grad = step_tiles(1, ids, picked, columns, counts)
    held = call(hold_half_kernel, HELD, specs=[SMEM] + [VMEM] * 2, n_after=1)(
        y, own, block_sums, near_grad
    )
    held = next_stratum(held)
    table, bias, sums, bias_sums = row_update(
        1, True, *grads, table, bias, sums, bias_sums, pick_col, pick_row
    )
    mine, theirs, _ = call(
        split_sum_kernel,
        (CODED_HALF, CODED_HALF, CODED),
        size=1 << 20,
        specs=[SMEM] + [VMEM] * 5,
    )(y, *reduce_columns(part, (bias, held)))
    new_block, new_bias, new_sums, new_bias_sums = call(
        last_update_kernel,
        (
            shape((SHARD, K), BF16),
            shape((1, SHARD), BF16),
            shape((SHARD, K), F32),
            shape((1, SHARD), F32),
        ),
        size=1 << 20,
        specs=[SMEM] + [VMEM] * 3,
    )(y, next_stratum(mine), next_stratum_swap_y(theirs), held)
    return (
        table,
        bias.reshape(RTAB),
        sums,
        bias_sums.reshape(RTAB),
        new_block,
        new_bias.reshape(SHARD),
        new_sums,
        new_bias_sums.reshape(SHARD),
    )


def solution(mesh):
    both = P(("stratum", "group"))
    rows = P(("stratum", "group"), None)
    in_specs = (
        rows,
        both,
        rows,
        both,
        rows,
        both,
        rows,
        both,
        P("stratum", "group", None, None),
        P("stratum", "group", None, None, None),
    )
    out_specs = (rows, both, rows, both, rows, both, rows, both)
    return jax.shard_map(shards, mesh=mesh, in_specs=in_specs, out_specs=out_specs, check_vma=False)
```

```python
import functools

import jax
import jax.numpy as jnp
from jax import lax
from jax.experimental import pallas as pl
from jax.experimental.pallas import tpu as pltpu
from jax.sharding import PartitionSpec as P

LEARN_RATE = 0.2
COUNT_CAP = 100.0
POWER = 0.75

K = 256
BATCH = 512
RTAB = 1024
SHARD = 128
PIECE = 256
PIECE_B = PIECE + 16
PIECE_F = PIECE + 8
SHARD_B = SHARD + 16
SHARD_F = SHARD + 8
NZ = 8
NY = 2

F32 = jnp.float32
BF16 = jnp.bfloat16
VMEM = pl.BlockSpec(memory_space=pltpu.VMEM)
SMEM = pl.BlockSpec(memory_space=pltpu.SMEM)


ANY = pl.BlockSpec(memory_space=pl.ANY)


def call(kernel, out_shape, flops=0, size=0, specs=None, n_in=0, n_after=0):
    specs = specs or [VMEM] * n_in
    n_read = len(specs)

    def body(*refs):
        kernel(*refs[:n_read], *refs[n_read + n_after :])

    return pl.pallas_call(
        body,
        out_shape=out_shape,
        in_specs=specs + [ANY] * n_after,
        out_specs=jax.tree.map(lambda _: VMEM, out_shape),
        cost_estimate=pl.CostEstimate(flops=0, bytes_accessed=0, transcendentals=0),
        compiler_params=pltpu.CompilerParams(vmem_limit_bytes=16 * 1024 * 1024),
    )


def shape(dims, dtype):
    return jax.ShapeDtypeStruct(dims, dtype)


def along_z(block, distance):
    group = NZ * NY
    route = []
    for s in range(lax.axis_size("stratum")):
        step = distance if s % 2 == 0 else -distance
        for g in range(group):
            route.append((s * group + g, s * group + ((g // NY + step) % NZ) * NY + g % NY))
    return lax.ppermute(block, ("stratum", "group"), route)


def swap_y(block):
    return lax.ppermute(block, "group", [(g, g ^ 1) for g in range(NZ * NY)])


def next_stratum(block):
    size = lax.axis_size("stratum")
    return lax.ppermute(block, "stratum", [(s, (s + 1) % size) for s in range(size)])


def next_stratum_swap_y(block):
    size = lax.axis_size("stratum")
    group = NZ * NY
    route = [
        (s * group + g, ((s + 1) % size) * group + (g ^ 1)) for s in range(size) for g in range(group)
    ]
    return lax.ppermute(block, ("stratum", "group"), route)


GRAIN = 700.0
REACH = 32760.0


def scale_code(top):
    return jnp.floor(jnp.log(jnp.maximum(top, 1e-18)) * GRAIN) + 2.0


def nearest(values):
    return jnp.clip(jnp.floor(values + 0.5), -32767.0, 32767.0).astype(jnp.int32).astype(jnp.int16)


def encode(grad, bias_grad):
    code = scale_code(jnp.max(jnp.abs(grad), axis=1, keepdims=True))
    data = nearest(grad * (jnp.exp(code * (-1.0 / GRAIN)) * REACH))
    codes = jnp.broadcast_to(code, (PIECE, 128)).T[:1]
    bias_code = scale_code(jnp.max(jnp.abs(bias_grad), axis=1, keepdims=True))
    scaled = bias_grad * (jnp.exp(bias_code * (-1.0 / GRAIN)) * REACH)
    high = jnp.floor(scaled + 0.5)
    low = (scaled - high) * REACH
    row = lax.broadcasted_iota(jnp.int32, (16, K), 0)
    tail = jnp.where(row == 0, high, jnp.where(row == 1, low, jnp.where(row == 2, bias_code, codes)))
    return data, nearest(tail)


def decode_rows(data, codes):
    scale = jnp.exp(codes * (1.0 / GRAIN)) * (1.0 / REACH)
    scale = jnp.broadcast_to(scale, (128, codes.shape[1])).T
    return data.astype(jnp.int32).astype(F32) * jnp.concatenate([scale, scale], axis=1)


def wide(tail):
    return tail.astype(jnp.int32).astype(F32)


def decode_bias(tail):
    scale = jnp.exp(tail[2:3] * (1.0 / GRAIN)) * (1.0 / REACH)
    return (tail[0:1] + tail[1:2] * (1.0 / REACH)) * scale


def decode(ref):
    tail = wide(ref[PIECE:])
    return decode_rows(ref[:PIECE], tail[3:4]), decode_bias(tail)


CODED = jax.ShapeDtypeStruct((PIECE_B, K), jnp.int16)
CODED_HALF = jax.ShapeDtypeStruct((SHARD_B, K), jnp.int16)


def store_coded(grad, bias_grad, out_ref):
    data, tail = encode(grad, bias_grad)
    out_ref[:PIECE] = data
    out_ref[PIECE:] = tail


def pack_kernel(rows_ref, bias_ref, out_ref):
    out_ref[:SHARD] = rows_ref[...]
    pad = out_ref.shape[0] - SHARD
    out_ref[SHARD:] = jnp.zeros((pad, K), out_ref.dtype)
    wide = jnp.concatenate([bias_ref[...], bias_ref[...]], axis=1).astype(F32)
    row = lax.broadcasted_iota(jnp.int32, (pad, K), 0)
    out_ref[SHARD:] = jnp.where(row == 0, jnp.broadcast_to(wide, (pad, K)), 0.0).astype(out_ref.dtype)


def pack(rows, bias):
    pad = 16 if rows.dtype == BF16 else 8
    return call(pack_kernel, shape((SHARD + pad, K), rows.dtype), n_in=2)(rows, bias.reshape(1, SHARD))


def merge_kernel(y_ref, own_ref, other_ref, out_ref):
    y = y_ref[0]
    mine = pl.multiple_of(y * SHARD, SHARD)
    theirs = pl.multiple_of((1 - y) * SHARD, SHARD)
    out_ref[pl.ds(mine, SHARD)] = own_ref[:SHARD]
    out_ref[pl.ds(theirs, SHARD)] = other_ref[:SHARD]
    a = own_ref[SHARD:].astype(F32)
    b = other_ref[SHARD:].astype(F32)
    lane = lax.broadcasted_iota(jnp.int32, a.shape, 1)
    out_ref[PIECE:] = jnp.where((lane < SHARD) == (y == 0), a, b).astype(out_ref.dtype)


def merge(y, own, other, after):
    return call(
        merge_kernel, shape((PIECE_B, K), BF16), specs=[SMEM, VMEM, VMEM], n_after=len(after)
    )(y, own, other, *after)


HELD = jax.ShapeDtypeStruct((SHARD_F, 2 * K), F32)


def hold_kernel(block_ref, bias_ref, sums_ref, bias_sums_ref, out_ref):
    out_ref[:SHARD, :K] = block_ref[...].astype(F32)
    out_ref[:SHARD, K:] = sums_ref[...]
    both = [bias_ref[...].astype(F32)] * 2 + [bias_sums_ref[...]] * 2
    out_ref[SHARD:] = jnp.broadcast_to(jnp.concatenate(both, axis=1), (8, 2 * K))


def hold_half_kernel(y_ref, block_ref, sums_ref, out_ref):
    y = y_ref[0]
    mine = pl.multiple_of(y * SHARD, SHARD)
    out_ref[:SHARD, :K] = block_ref[pl.ds(mine, SHARD)].astype(F32)
    out_ref[:SHARD, K:] = sums_ref[pl.ds(mine, SHARD)]
    both = []
    for tail in (block_ref[PIECE:].astype(F32)[:1], sums_ref[PIECE:][:1]):
        both += [jnp.where(y == 0, tail[:, :SHARD], tail[:, SHARD:])] * 2
    out_ref[SHARD:] = jnp.broadcast_to(jnp.concatenate(both, axis=1), (8, 2 * K))


def column_of(picks):
    return jnp.broadcast_to(picks.astype(F32), (128, BATCH)).T[:, :1].astype(jnp.int32)


def pick_rows(table, bias, pick_col, picked_ref, picked_bias_ref):
    lane = lax.broadcasted_iota(jnp.int32, (BATCH, RTAB), 1)
    hot = lane == pick_col
    one_hot = jnp.where(hot, 1.0, 0.0).astype(BF16)
    picked_ref[...] = jnp.dot(one_hot, table, preferred_element_type=F32).astype(BF16)
    column = jnp.sum(jnp.where(hot, bias, 0.0), axis=1, keepdims=True)
    picked_bias_ref[...] = jnp.broadcast_to(column, (BATCH, 128))


def gather_kernel(table_ref, bias_ref, pick_ref, picked_ref, picked_bias_ref):
    pick_col = column_of(pick_ref[:1])
    pick_rows(table_ref[...], bias_ref[...].astype(F32), pick_col, picked_ref, picked_bias_ref)


PICKED = (shape((BATCH, K), BF16), shape((BATCH, 128), F32))


def gather(table, bias, pick_row):
    return call(gather_kernel, PICKED, n_in=3)(
        table, bias, pick_row
    )


def row_update_kernel(
    step,
    grad_refs,
    bias_grad_refs,
    table_ref,
    bias_ref,
    sums_ref,
    bias_sums_ref,
    pick_row_ref,
    table_out,
    bias_out,
    sums_out,
    bias_sums_out,
    *picked_refs,
):
    grad = grad_refs[...]
    high = grad.astype(BF16)
    rest = grad - high.astype(F32)
    middle = rest.astype(BF16)
    low = (rest - middle.astype(F32)).astype(BF16)
    parts = jnp.concatenate([high, middle, low], axis=1)
    chunk = 256
    for c in range(RTAB // chunk):
        rows = slice(c * chunk, (c + 1) * chunk)
        index = lax.broadcasted_iota(jnp.int32, (chunk, BATCH), 0) + c * chunk
        spread = jnp.where(index == pick_row_ref[step : step + 1, :], 1.0, 0.0).astype(BF16)
        moved = jnp.dot(spread, parts, preferred_element_type=F32)
        full = moved[:, :K] + moved[:, K : 2 * K] + moved[:, 2 * K :]
        new_sums = sums_ref[rows] + full * full
        sums_out[rows] = new_sums
        table_out[rows] = (
            table_ref[rows].astype(F32) - LEARN_RATE * full * lax.rsqrt(new_sums)
        ).astype(BF16)
    column = jnp.sum(bias_grad_refs[...], axis=1, keepdims=True)
    lane = lax.broadcasted_iota(jnp.int32, (BATCH, RTAB), 1)
    hot = lane == column_of(pick_row_ref[step : step + 1])
    bias_grad = jnp.sum(jnp.where(hot, column, 0.0), axis=0, keepdims=True)
    new_bias_sums = bias_sums_ref[...] + bias_grad * bias_grad
    bias_sums_out[...] = new_bias_sums
    new_bias = (
        bias_ref[...].astype(F32) - LEARN_RATE * bias_grad * lax.rsqrt(new_bias_sums)
    ).astype(BF16)
    bias_out[...] = new_bias
    if picked_refs:
        pick_col = column_of(pick_row_ref[step + 1 : step + 2])
        pick_rows(table_out[...], new_bias.astype(F32), pick_col, *picked_refs)


def row_update(step, last, grad, bias_grad, table, bias, sums, bias_sums, pick_row):
    outs = (
        shape((RTAB, K), BF16),
        shape((1, RTAB), BF16),
        shape((RTAB, K), F32),
        shape((1, RTAB), F32),
    )
    if not last:
        outs = outs + PICKED
    return call(
        functools.partial(row_update_kernel, step),
        outs,
        flops=8 * BATCH * RTAB * K,
        size=5 << 20,
        n_in=7,
    )(grad, bias_grad, table, bias, sums, bias_sums, pick_row)


def tile_kernel(offsets, first, n_after, *refs):
    refs = list(refs)
    n = len(offsets)
    refs.pop(0)
    picked_ref, picked_bias_ref = refs.pop(0), refs.pop(0)
    columns = [refs.pop(0) for _ in range(n)]
    counts = [refs.pop(0) for _ in range(n)]
    if not first:
        grad_in, bias_in = refs.pop(0), refs.pop(0)
    refs = refs[n_after:]
    grad_out, bias_out = refs.pop(0), refs.pop(0)
    picked = picked_ref[...]
    picked_bias = jnp.concatenate([picked_bias_ref[...]] * 2, axis=1)
    row_grad = None if first else grad_in[...]
    row_bias_grad = None if first else bias_in[...]
    for i in range(n):
        block, tail = columns[i][:PIECE], columns[i][PIECE:]
        bias = tail.astype(F32)[:1]
        scores = lax.dot_general(
            picked, block, (((1,), (1,)), ((), ())), preferred_element_type=F32
        )
        scores = scores + picked_bias + bias
        counted = counts[i][...].astype(F32)
        target = jnp.log(jnp.maximum(counted, 1.0))
        weight = jnp.exp(POWER * target - POWER * jnp.log(jnp.float32(COUNT_CAP)))
        weight = jnp.where(counted > 0.0, jnp.minimum(weight, 1.0), 0.0)
        residual = weight * (scores - target)
        half = residual.astype(BF16)
        part = jnp.dot(half, block, preferred_element_type=F32)
        row_grad = part if row_grad is None else row_grad + part
        lanes = residual[:, :128] + residual[:, 128:]
        row_bias_grad = lanes if row_bias_grad is None else row_bias_grad + lanes
        col_grad = lax.dot_general(
            half, picked, (((0,), (0,)), ((), ())), preferred_element_type=F32
        )
        bias_grad = jnp.sum(residual, axis=0, keepdims=True)
        if offsets[i] in LOCAL:
            out = refs.pop(0)
            out[:PIECE] = col_grad
            out[PIECE:] = jnp.broadcast_to(bias_grad, (PIECE_F - PIECE, K))
        else:
            store_coded(col_grad, bias_grad, refs.pop(0))
    grad_out[...] = row_grad
    bias_out[...] = row_bias_grad


LOCAL = (0, 2, -2)


def tiles(step, offsets, ids, picked, columns, counts, grads, after=()):
    n = len(offsets)
    first = grads is None

    def whole(dims):
        return pl.BlockSpec(dims, lambda i, ids: (0, 0))

    specs = [whole((BATCH, K)), whole((BATCH, 128))]
    specs += [whole(c.shape) for c in columns]
    for offset in offsets:
        specs.append(
            pl.BlockSpec(
                (None, None, None, BATCH, PIECE),
                functools.partial(lambda at, i, ids: (0, 0, step, 0, ids[at]), offset % NZ),
            )
        )
    args = [*picked, *columns, *([counts] * n)]
    if not first:
        specs += [whole((BATCH, K)), whole((BATCH, 128))]
        args += list(grads)
    specs += [ANY] * len(after)
    args += list(after)
    out_shape = [shape((BATCH, K), F32), shape((BATCH, 128), F32)]
    for offset in offsets:
        if offset in LOCAL:
            out_shape.append(shape((PIECE_F, K), F32))
        else:
            out_shape.append(CODED)
    out_specs = [whole(o.shape) for o in out_shape]
    outs = pl.pallas_call(
        functools.partial(tile_kernel, offsets, first, len(after)),
        grid_spec=pltpu.PrefetchScalarGridSpec(
            num_scalar_prefetch=1, grid=(1,), in_specs=specs, out_specs=out_specs
        ),
        out_shape=out_shape,
        cost_estimate=pl.CostEstimate(flops=0, bytes_accessed=0, transcendentals=0),
        compiler_params=pltpu.CompilerParams(vmem_limit_bytes=24 * 1024 * 1024),
    )(ids, *args)
    return dict(zip(offsets, outs[2:])), tuple(outs[:2])


def relay_kernel(up_ref, down_ref, up3_ref, down3_ref, up4_ref, up_out, down_out):
    store_coded(*column_total(up_ref, (up3_ref, up4_ref)), up_out)
    store_coded(*column_total(down_ref, (down3_ref,)), down_out)


def column_total(own_ref, refs):
    grad, bias_grad = own_ref[:PIECE], own_ref[PIECE:][:1]
    for ref in refs:
        more, more_bias = decode(ref)
        grad, bias_grad = grad + more, bias_grad + more_bias
    return grad, bias_grad


def sum_kernel(own_ref, a, b, c, d, out):
    store_coded(*column_total(own_ref, (a, b, c, d)), out)


def split_sum_kernel(y_ref, own_ref, a, b, c, d, mine_out, theirs_out):
    grad, bias_grad = column_total(own_ref, (a, b, c, d))
    low, high = grad[:SHARD], grad[SHARD:]
    even = y_ref[0] == 0
    mine, theirs = jnp.where(even, low, high), jnp.where(even, high, low)
    data, tail = encode(jnp.concatenate([mine, theirs], axis=0), bias_grad)
    mine_out[:SHARD] = data[:SHARD]
    theirs_out[:SHARD] = data[SHARD:]
    mine_out[SHARD:] = tail
    theirs_out[SHARD:] = tail


def gather_columns(own):
    up1, down1 = along_z(own, -1), along_z(own, 1)
    up2, down2 = along_z(own, -2), along_z(own, 2)
    up3, down3 = along_z(up2, -1), along_z(down2, 1)
    far = along_z(up2, -2)
    return {0: own, 1: up1, -1: down1, 2: up2, -2: down2, 3: up3, -3: down3, 4: far}


def reduce_columns(part, after):
    up3, down3 = along_z(part[3], 1), along_z(part[-3], -1)
    up4 = along_z(part[4], 2)
    near = [along_z(part[1], 1), along_z(part[-1], -1)]
    up2, down2 = call(relay_kernel, (CODED,) * 2, size=2 << 20, n_in=5, n_after=len(after))(
        part[2], part[-2], up3, down3, up4, *after
    )
    return [part[0], *near, along_z(up2, 2), along_z(down2, -2)]


def step_tiles(step, ids, picked, columns, counts):
    part = {}
    got, grads = tiles(step, [0], ids, picked, [columns[0]], counts, None)
    part.update(got)
    near = [1, -1, 2, -2]
    got, grads = tiles(step, near, ids, picked, [columns[d] for d in near], counts, grads)
    part.update(got)
    near_grad = grads[1]
    far = [3, -3, 4]
    far_columns = [columns[3], columns[-3], columns[4]]
    got, grads = tiles(step, far, ids, picked, far_columns, counts, grads)
    part.update(got)
    return part, grads, near_grad


def column_update_kernel(y_ref, a_ref, b_ref, held_a, held_b, block_out, sums_out):
    y = y_ref[0]
    grad, bias_grad = decode(a_ref)
    more, more_bias = decode(b_ref)
    grad, bias_grad = grad + more, bias_grad + more_bias
    tails = [held_a[SHARD:][:1], held_b[SHARD:][:1]]
    for half in range(2):
        rows = slice(half * SHARD, (half + 1) * SHARD)
        held = jnp.where(y == half, held_a[:SHARD], held_b[:SHARD])
        new_sums = held[:, K:] + grad[rows] * grad[rows]
        sums_out[rows] = new_sums
        block_out[rows] = (
            held[:, :K] - LEARN_RATE * grad[rows] * lax.rsqrt(new_sums)
        ).astype(BF16)
    lane = lax.broadcasted_iota(jnp.int32, (1, 2 * K), 1) % K
    tail = jnp.where((lane < SHARD) == (y == 0), tails[0], tails[1])
    bias_sums = tail[:, K:] + bias_grad * bias_grad
    bias = tail[:, :K] - LEARN_RATE * bias_grad * lax.rsqrt(bias_sums)
    row = lax.broadcasted_iota(jnp.int32, (8, K), 0)
    sums_out[PIECE:] = jnp.where(row == 0, bias_sums, 0.0)
    row = lax.broadcasted_iota(jnp.int32, (16, K), 0)
    block_out[PIECE:] = jnp.where(row == 0, bias, 0.0).astype(BF16)


def last_update_kernel(
    y_ref, a_ref, b_ref, held_ref, block_out, bias_out, sums_out, bias_sums_out
):
    y = y_ref[0]
    grad, bias_grad = 0.0, 0.0
    for ref, lanes in ((a_ref, slice(0, SHARD)), (b_ref, slice(SHARD, K))):
        tail = wide(ref[SHARD:])
        codes = tail[3:4, lanes]
        grad = grad + decode_rows(ref[:SHARD], codes)
        bias_grad = bias_grad + decode_bias(tail)
    bias_grad = jnp.where(y == 0, bias_grad[:, :SHARD], bias_grad[:, SHARD:])
    new_sums = held_ref[:SHARD, K:] + grad * grad
    sums_out[...] = new_sums
    block_out[...] = (
        held_ref[:SHARD, :K] - LEARN_RATE * grad * lax.rsqrt(new_sums)
    ).astype(BF16)
    tail = held_ref[SHARD:][:1]
    bias_sums = tail[:, K : K + SHARD] + bias_grad * bias_grad
    bias_sums_out[...] = bias_sums
    bias_out[...] = (tail[:, :SHARD] - LEARN_RATE * bias_grad * lax.rsqrt(bias_sums)).astype(BF16)


def shards(
    row_factors,
    row_bias,
    row_sums,
    row_bias_sums,
    col_factors,
    col_bias,
    col_sums,
    col_bias_sums,
    row_pick,
    counts,
):
    at = lax.axis_index("group")
    y = (at % NY).astype(jnp.int32).reshape(1)
    way = 1 - 2 * (lax.axis_index("stratum") % 2)
    ids = ((at // NY + way * jnp.arange(NZ) + NZ) % NZ).astype(jnp.int32)

    own_shard = pack(col_factors, col_bias)
    other_shard = swap_y(own_shard)
    pick_row = row_pick[0, 0]
    table, bias, sums, bias_sums = (
        row_factors,
        row_bias.reshape(1, RTAB),
        row_sums,
        row_bias_sums.reshape(1, RTAB),
    )
    picked = gather(table, bias, pick_row)
    own = merge(y, own_shard, other_shard, (picked[0],))
    columns = gather_columns(own)

    part, grads, near_grad = step_tiles(0, ids, picked, columns, counts)
    held = call(hold_kernel, HELD, n_in=4, n_after=1)(
        col_factors, col_bias.reshape(1, SHARD), col_sums, col_bias_sums.reshape(1, SHARD), near_grad
    )
    held = (next_stratum(held), next_stratum_swap_y(held))
    table, bias, sums, bias_sums, *picked = row_update(
        0, False, *grads, table, bias, sums, bias_sums, pick_row
    )
    total = call(sum_kernel, CODED, size=1 << 20, n_in=5)(*reduce_columns(part, (picked[0], *held)))
    own, block_sums = call(
        column_update_kernel,
        (shape((PIECE_B, K), BF16), shape((PIECE_F, K), F32)),
        size=2 << 20,
        specs=[SMEM] + [VMEM] * 4,
    )(y, next_stratum(total), next_stratum_swap_y(total), *held)

    columns = gather_columns(own)
    part, grads, near_grad = step_tiles(1, ids, picked, columns, counts)
    held = call(hold_half_kernel, HELD, specs=[SMEM] + [VMEM] * 2, n_after=1)(
        y, own, block_sums, near_grad
    )
    held = next_stratum(held)
    table, bias, sums, bias_sums = row_update(
        1, True, *grads, table, bias, sums, bias_sums, pick_row
    )
    mine, theirs = call(
        split_sum_kernel,
        (CODED_HALF, CODED_HALF),
        size=1 << 20,
        specs=[SMEM] + [VMEM] * 5,
    )(y, *reduce_columns(part, (bias, held)))
    new_block, new_bias, new_sums, new_bias_sums = call(
        last_update_kernel,
        (
            shape((SHARD, K), BF16),
            shape((1, SHARD), BF16),
            shape((SHARD, K), F32),
            shape((1, SHARD), F32),
        ),
        size=1 << 20,
        specs=[SMEM] + [VMEM] * 3,
    )(y, next_stratum(mine), next_stratum_swap_y(theirs), held)
    return (
        table,
        bias.reshape(RTAB),
        sums,
        bias_sums.reshape(RTAB),
        new_block,
        new_bias.reshape(SHARD),
        new_sums,
        new_bias_sums.reshape(SHARD),
    )


def solution(mesh):
    both = P(("stratum", "group"))
    rows = P(("stratum", "group"), None)
    in_specs = (
        rows,
        both,
        rows,
        both,
        rows,
        both,
        rows,
        both,
        P("stratum", "group", None, None),
        P("stratum", "group", None, None, None),
    )
    out_specs = (rows, both, rows, both, rows, both, rows, both)
    return jax.shard_map(shards, mesh=mesh, in_specs=in_specs, out_specs=out_specs, check_vma=False)
```

```python
import functools

import jax
import jax.numpy as jnp
from jax import lax
from jax.experimental import pallas as pl
from jax.experimental.pallas import tpu as pltpu
from jax.sharding import PartitionSpec as P

LEARN_RATE = 0.2
COUNT_CAP = 100.0
POWER = 0.75

K = 256
BATCH = 512
RTAB = 1024
SHARD = 128
PIECE = 256
PIECE_B = PIECE + 16
PIECE_F = PIECE + 8
SHARD_B = SHARD + 16
SHARD_F = SHARD + 8
NZ = 8
NY = 2

F32 = jnp.float32
BF16 = jnp.bfloat16
VMEM = pl.BlockSpec(memory_space=pltpu.VMEM)
SMEM = pl.BlockSpec(memory_space=pltpu.SMEM)


ANY = pl.BlockSpec(memory_space=pl.ANY)


def call(kernel, out_shape, flops=0, size=0, specs=None, n_in=0, n_after=0):
    specs = specs or [VMEM] * n_in
    n_read = len(specs)

    def body(*refs):
        kernel(*refs[:n_read], *refs[n_read + n_after :])

    return pl.pallas_call(
        body,
        out_shape=out_shape,
        in_specs=specs + [ANY] * n_after,
        out_specs=jax.tree.map(lambda _: VMEM, out_shape),
        cost_estimate=pl.CostEstimate(flops=0, bytes_accessed=0, transcendentals=0),
        compiler_params=pltpu.CompilerParams(vmem_limit_bytes=16 * 1024 * 1024),
    )


def shape(dims, dtype):
    return jax.ShapeDtypeStruct(dims, dtype)


def along_z(block, distance):
    group = NZ * NY
    route = []
    for s in range(lax.axis_size("stratum")):
        step = distance if s % 2 == 0 else -distance
        for g in range(group):
            route.append((s * group + g, s * group + ((g // NY + step) % NZ) * NY + g % NY))
    return lax.ppermute(block, ("stratum", "group"), route)


def swap_y(block):
    return lax.ppermute(block, "group", [(g, g ^ 1) for g in range(NZ * NY)])


def next_stratum(block):
    size = lax.axis_size("stratum")
    return lax.ppermute(block, "stratum", [(s, (s + 1) % size) for s in range(size)])


def next_stratum_swap_y(block):
    size = lax.axis_size("stratum")
    group = NZ * NY
    route = [
        (s * group + g, ((s + 1) % size) * group + (g ^ 1)) for s in range(size) for g in range(group)
    ]
    return lax.ppermute(block, ("stratum", "group"), route)


GRAIN = 700.0
REACH = 32760.0


def scale_code(top):
    return jnp.floor(jnp.log(jnp.maximum(top, 1e-18)) * GRAIN) + 2.0


def nearest(values):
    return jnp.clip(jnp.floor(values + 0.5), -32767.0, 32767.0).astype(jnp.int32).astype(jnp.int16)


def encode(grad, bias_grad):
    code = scale_code(jnp.max(jnp.abs(grad), axis=1, keepdims=True))
    data = nearest(grad * (jnp.exp(code * (-1.0 / GRAIN)) * REACH))
    codes = jnp.broadcast_to(code, (PIECE, 128)).T[:1]
    bias_code = scale_code(jnp.max(jnp.abs(bias_grad), axis=1, keepdims=True))
    scaled = bias_grad * (jnp.exp(bias_code * (-1.0 / GRAIN)) * REACH)
    high = jnp.floor(scaled + 0.5)
    low = (scaled - high) * REACH
    row = lax.broadcasted_iota(jnp.int32, (16, K), 0)
    tail = jnp.where(row == 0, high, jnp.where(row == 1, low, jnp.where(row == 2, bias_code, codes)))
    return data, nearest(tail)


def decode_rows(data, codes):
    scale = jnp.exp(codes * (1.0 / GRAIN)) * (1.0 / REACH)
    scale = jnp.broadcast_to(scale, (128, codes.shape[1])).T
    return data.astype(jnp.int32).astype(F32) * jnp.concatenate([scale, scale], axis=1)


def wide(tail):
    return tail.astype(jnp.int32).astype(F32)


def decode_bias(tail):
    scale = jnp.exp(tail[2:3] * (1.0 / GRAIN)) * (1.0 / REACH)
    return (tail[0:1] + tail[1:2] * (1.0 / REACH)) * scale


def decode(ref):
    tail = wide(ref[PIECE:])
    return decode_rows(ref[:PIECE], tail[3:4]), decode_bias(tail)


CODED = jax.ShapeDtypeStruct((PIECE_B, K), jnp.int16)
CODED_HALF = jax.ShapeDtypeStruct((SHARD_B, K), jnp.int16)


def store_coded(grad, bias_grad, out_ref):
    data, tail = encode(grad, bias_grad)
    out_ref[:PIECE] = data
    out_ref[PIECE:] = tail


def pack(rows, bias):
    tail = jnp.pad(jnp.tile(bias, 2)[None], ((0, SHARD_B - SHARD - 1), (0, 0)))
    return jnp.concatenate([rows, tail], axis=0)


def merge_kernel(y_ref, own_ref, other_ref, out_ref):
    y = y_ref[0]
    mine = pl.multiple_of(y * SHARD, SHARD)
    theirs = pl.multiple_of((1 - y) * SHARD, SHARD)
    out_ref[pl.ds(mine, SHARD)] = own_ref[:SHARD]
    out_ref[pl.ds(theirs, SHARD)] = other_ref[:SHARD]
    a = own_ref[SHARD:].astype(F32)
    b = other_ref[SHARD:].astype(F32)
    lane = lax.broadcasted_iota(jnp.int32, a.shape, 1)
    out_ref[PIECE:] = jnp.where((lane < SHARD) == (y == 0), a, b).astype(out_ref.dtype)


def merge(y, own, other, after):
    return call(
        merge_kernel, shape((PIECE_B, K), BF16), specs=[SMEM, VMEM, VMEM], n_after=len(after)
    )(y, own, other, *after)


HELD = jax.ShapeDtypeStruct((SHARD_F, 2 * K), F32)


def hold_kernel(block_ref, bias_ref, sums_ref, bias_sums_ref, out_ref):
    out_ref[:SHARD, :K] = block_ref[...].astype(F32)
    out_ref[:SHARD, K:] = sums_ref[...]
    both = [bias_ref[...].astype(F32)] * 2 + [bias_sums_ref[...]] * 2
    out_ref[SHARD:] = jnp.broadcast_to(jnp.concatenate(both, axis=1), (8, 2 * K))


def hold_half_kernel(y_ref, block_ref, sums_ref, out_ref):
    y = y_ref[0]
    mine = pl.multiple_of(y * SHARD, SHARD)
    out_ref[:SHARD, :K] = block_ref[pl.ds(mine, SHARD)].astype(F32)
    out_ref[:SHARD, K:] = sums_ref[pl.ds(mine, SHARD)]
    both = []
    for tail in (block_ref[PIECE:].astype(F32)[:1], sums_ref[PIECE:][:1]):
        both += [jnp.where(y == 0, tail[:, :SHARD], tail[:, SHARD:])] * 2
    out_ref[SHARD:] = jnp.broadcast_to(jnp.concatenate(both, axis=1), (8, 2 * K))


def column_of(picks):
    return jnp.broadcast_to(picks.astype(F32), (128, BATCH)).T[:, :1].astype(jnp.int32)


def pick_rows(table, bias, pick_col, picked_ref, picked_bias_ref):
    lane = lax.broadcasted_iota(jnp.int32, (BATCH, RTAB), 1)
    hot = lane == pick_col
    one_hot = jnp.where(hot, 1.0, 0.0).astype(BF16)
    picked_ref[...] = jnp.dot(one_hot, table, preferred_element_type=F32).astype(BF16)
    column = jnp.sum(jnp.where(hot, bias, 0.0), axis=1, keepdims=True)
    picked_bias_ref[...] = jnp.broadcast_to(column, (BATCH, 128))


def gather_kernel(table_ref, bias_ref, pick_ref, picked_ref, picked_bias_ref):
    pick_col = column_of(pick_ref[:1])
    pick_rows(table_ref[...], bias_ref[...].astype(F32), pick_col, picked_ref, picked_bias_ref)


PICKED = (shape((BATCH, K), BF16), shape((BATCH, 128), F32))


def gather(table, bias, pick_row):
    return call(gather_kernel, PICKED, n_in=3)(
        table, bias, pick_row
    )


def row_update_kernel(
    step,
    grad_refs,
    bias_grad_refs,
    table_ref,
    bias_ref,
    sums_ref,
    bias_sums_ref,
    pick_row_ref,
    table_out,
    bias_out,
    sums_out,
    bias_sums_out,
    *picked_refs,
):
    grad = grad_refs[...]
    high = grad.astype(BF16)
    rest = grad - high.astype(F32)
    middle = rest.astype(BF16)
    low = (rest - middle.astype(F32)).astype(BF16)
    parts = jnp.concatenate([high, middle, low], axis=1)
    chunk = 256
    for c in range(RTAB // chunk):
        rows = slice(c * chunk, (c + 1) * chunk)
        index = lax.broadcasted_iota(jnp.int32, (chunk, BATCH), 0) + c * chunk
        spread = jnp.where(index == pick_row_ref[step : step + 1, :], 1.0, 0.0).astype(BF16)
        moved = jnp.dot(spread, parts, preferred_element_type=F32)
        full = moved[:, :K] + moved[:, K : 2 * K] + moved[:, 2 * K :]
        new_sums = sums_ref[rows] + full * full
        sums_out[rows] = new_sums
        table_out[rows] = (
            table_ref[rows].astype(F32) - LEARN_RATE * full * lax.rsqrt(new_sums)
        ).astype(BF16)
    column = jnp.sum(bias_grad_refs[...], axis=1, keepdims=True)
    lane = lax.broadcasted_iota(jnp.int32, (BATCH, RTAB), 1)
    hot = lane == column_of(pick_row_ref[step : step + 1])
    bias_grad = jnp.sum(jnp.where(hot, column, 0.0), axis=0, keepdims=True)
    new_bias_sums = bias_sums_ref[...] + bias_grad * bias_grad
    bias_sums_out[...] = new_bias_sums
    new_bias = (
        bias_ref[...].astype(F32) - LEARN_RATE * bias_grad * lax.rsqrt(new_bias_sums)
    ).astype(BF16)
    bias_out[...] = new_bias
    if picked_refs:
        pick_col = column_of(pick_row_ref[step + 1 : step + 2])
        pick_rows(table_out[...], new_bias.astype(F32), pick_col, *picked_refs)


def row_update(step, last, grad, bias_grad, table, bias, sums, bias_sums, pick_row):
    outs = (
        shape((RTAB, K), BF16),
        shape((1, RTAB), BF16),
        shape((RTAB, K), F32),
        shape((1, RTAB), F32),
    )
    if not last:
        outs = outs + PICKED
    return call(
        functools.partial(row_update_kernel, step),
        outs,
        flops=8 * BATCH * RTAB * K,
        size=5 << 20,
        n_in=7,
    )(grad, bias_grad, table, bias, sums, bias_sums, pick_row)


def tile_kernel(offsets, first, n_after, *refs):
    refs = list(refs)
    n = len(offsets)
    refs.pop(0)
    picked_ref, picked_bias_ref = refs.pop(0), refs.pop(0)
    columns = [refs.pop(0) for _ in range(n)]
    counts = [refs.pop(0) for _ in range(n)]
    if not first:
        grad_in, bias_in = refs.pop(0), refs.pop(0)
    refs = refs[n_after:]
    grad_out, bias_out = refs.pop(0), refs.pop(0)
    picked = picked_ref[...]
    picked_bias = jnp.concatenate([picked_bias_ref[...]] * 2, axis=1)
    row_grad = None if first else grad_in[...]
    row_bias_grad = None if first else bias_in[...]
    for i in range(n):
        block, tail = columns[i][:PIECE], columns[i][PIECE:]
        bias = tail.astype(F32)[:1]
        scores = lax.dot_general(
            picked, block, (((1,), (1,)), ((), ())), preferred_element_type=F32
        )
        scores = scores + picked_bias + bias
        counted = counts[i][...].astype(F32)
        target = jnp.log(jnp.maximum(counted, 1.0))
        weight = jnp.exp(POWER * target - POWER * jnp.log(jnp.float32(COUNT_CAP)))
        weight = jnp.where(counted > 0.0, jnp.minimum(weight, 1.0), 0.0)
        residual = weight * (scores - target)
        half = residual.astype(BF16)
        part = jnp.dot(half, block, preferred_element_type=F32)
        row_grad = part if row_grad is None else row_grad + part
        lanes = residual[:, :128] + residual[:, 128:]
        row_bias_grad = lanes if row_bias_grad is None else row_bias_grad + lanes
        col_grad = lax.dot_general(
            half, picked, (((0,), (0,)), ((), ())), preferred_element_type=F32
        )
        bias_grad = jnp.sum(residual, axis=0, keepdims=True)
        if offsets[i] in LOCAL:
            out = refs.pop(0)
            out[:PIECE] = col_grad
            out[PIECE:] = jnp.broadcast_to(bias_grad, (PIECE_F - PIECE, K))
        else:
            store_coded(col_grad, bias_grad, refs.pop(0))
    grad_out[...] = row_grad
    bias_out[...] = row_bias_grad


LOCAL = (0, 2, -2)


def tiles(step, offsets, ids, picked, columns, counts, grads, after=()):
    n = len(offsets)
    first = grads is None

    def whole(dims):
        return pl.BlockSpec(dims, lambda i, ids: (0, 0))

    specs = [whole((BATCH, K)), whole((BATCH, 128))]
    specs += [whole(c.shape) for c in columns]
    for offset in offsets:
        specs.append(
            pl.BlockSpec(
                (None, None, None, BATCH, PIECE),
                functools.partial(lambda at, i, ids: (0, 0, step, 0, ids[at]), offset % NZ),
            )
        )
    args = [*picked, *columns, *([counts] * n)]
    if not first:
        specs += [whole((BATCH, K)), whole((BATCH, 128))]
        args += list(grads)
    specs += [ANY] * len(after)
    args += list(after)
    out_shape = [shape((BATCH, K), F32), shape((BATCH, 128), F32)]
    for offset in offsets:
        if offset in LOCAL:
            out_shape.append(shape((PIECE_F, K), F32))
        else:
            out_shape.append(CODED)
    out_specs = [whole(o.shape) for o in out_shape]
    outs = pl.pallas_call(
        functools.partial(tile_kernel, offsets, first, len(after)),
        grid_spec=pltpu.PrefetchScalarGridSpec(
            num_scalar_prefetch=1, grid=(1,), in_specs=specs, out_specs=out_specs
        ),
        out_shape=out_shape,
        cost_estimate=pl.CostEstimate(
            flops=n * 12 * BATCH * PIECE * K, bytes_accessed=n << 20, transcendentals=n << 18
        ),
        compiler_params=pltpu.CompilerParams(vmem_limit_bytes=24 * 1024 * 1024),
    )(ids, *args)
    return dict(zip(offsets, outs[2:])), tuple(outs[:2])


def relay_kernel(up_ref, down_ref, up3_ref, down3_ref, up4_ref, up_out, down_out):
    store_coded(*column_total(up_ref, (up3_ref, up4_ref)), up_out)
    store_coded(*column_total(down_ref, (down3_ref,)), down_out)


def column_total(own_ref, refs):
    grad, bias_grad = own_ref[:PIECE], own_ref[PIECE:][:1]
    for ref in refs:
        more, more_bias = decode(ref)
        grad, bias_grad = grad + more, bias_grad + more_bias
    return grad, bias_grad


def sum_kernel(own_ref, a, b, c, d, out):
    store_coded(*column_total(own_ref, (a, b, c, d)), out)


def split_sum_kernel(y_ref, own_ref, a, b, c, d, mine_out, theirs_out):
    grad, bias_grad = column_total(own_ref, (a, b, c, d))
    low, high = grad[:SHARD], grad[SHARD:]
    even = y_ref[0] == 0
    mine, theirs = jnp.where(even, low, high), jnp.where(even, high, low)
    data, tail = encode(jnp.concatenate([mine, theirs], axis=0), bias_grad)
    mine_out[:SHARD] = data[:SHARD]
    theirs_out[:SHARD] = data[SHARD:]
    mine_out[SHARD:] = tail
    theirs_out[SHARD:] = tail


def gather_columns(own):
    up1, down1 = along_z(own, -1), along_z(own, 1)
    up2, down2 = along_z(own, -2), along_z(own, 2)
    up3, down3 = along_z(up2, -1), along_z(down2, 1)
    far = along_z(up2, -2)
    return {0: own, 1: up1, -1: down1, 2: up2, -2: down2, 3: up3, -3: down3, 4: far}


def reduce_columns(part, after):
    up3, down3 = along_z(part[3], 1), along_z(part[-3], -1)
    up4 = along_z(part[4], 2)
    near = [along_z(part[1], 1), along_z(part[-1], -1)]
    up2, down2 = call(relay_kernel, (CODED,) * 2, size=2 << 20, n_in=5, n_after=len(after))(
        part[2], part[-2], up3, down3, up4, *after
    )
    return [part[0], *near, along_z(up2, 2), along_z(down2, -2)]


def step_tiles(step, ids, picked, columns, counts):
    part = {}
    got, grads = tiles(step, [0], ids, picked, [columns[0]], counts, None)
    part.update(got)
    near = [1, -1, 2, -2]
    got, grads = tiles(step, near, ids, picked, [columns[d] for d in near], counts, grads)
    part.update(got)
    near_grad = grads[1]
    far = [3, -3, 4]
    far_columns = [columns[3], columns[-3], columns[4]]
    got, grads = tiles(step, far, ids, picked, far_columns, counts, grads)
    part.update(got)
    return part, grads, near_grad


def column_update_kernel(y_ref, a_ref, b_ref, held_a, held_b, block_out, sums_out):
    y = y_ref[0]
    grad, bias_grad = decode(a_ref)
    more, more_bias = decode(b_ref)
    grad, bias_grad = grad + more, bias_grad + more_bias
    tails = [held_a[SHARD:][:1], held_b[SHARD:][:1]]
    for half in range(2):
        rows = slice(half * SHARD, (half + 1) * SHARD)
        held = jnp.where(y == half, held_a[:SHARD], held_b[:SHARD])
        new_sums = held[:, K:] + grad[rows] * grad[rows]
        sums_out[rows] = new_sums
        block_out[rows] = (
            held[:, :K] - LEARN_RATE * grad[rows] * lax.rsqrt(new_sums)
        ).astype(BF16)
    lane = lax.broadcasted_iota(jnp.int32, (1, 2 * K), 1) % K
    tail = jnp.where((lane < SHARD) == (y == 0), tails[0], tails[1])
    bias_sums = tail[:, K:] + bias_grad * bias_grad
    bias = tail[:, :K] - LEARN_RATE * bias_grad * lax.rsqrt(bias_sums)
    row = lax.broadcasted_iota(jnp.int32, (8, K), 0)
    sums_out[PIECE:] = jnp.where(row == 0, bias_sums, 0.0)
    row = lax.broadcasted_iota(jnp.int32, (16, K), 0)
    block_out[PIECE:] = jnp.where(row == 0, bias, 0.0).astype(BF16)


def last_update_kernel(
    y_ref, a_ref, b_ref, held_ref, block_out, bias_out, sums_out, bias_sums_out
):
    y = y_ref[0]
    grad, bias_grad = 0.0, 0.0
    for ref, lanes in ((a_ref, slice(0, SHARD)), (b_ref, slice(SHARD, K))):
        tail = wide(ref[SHARD:])
        codes = tail[3:4, lanes]
        grad = grad + decode_rows(ref[:SHARD], codes)
        bias_grad = bias_grad + decode_bias(tail)
    bias_grad = jnp.where(y == 0, bias_grad[:, :SHARD], bias_grad[:, SHARD:])
    new_sums = held_ref[:SHARD, K:] + grad * grad
    sums_out[...] = new_sums
    block_out[...] = (
        held_ref[:SHARD, :K] - LEARN_RATE * grad * lax.rsqrt(new_sums)
    ).astype(BF16)
    tail = held_ref[SHARD:][:1]
    bias_sums = tail[:, K : K + SHARD] + bias_grad * bias_grad
    bias_sums_out[...] = bias_sums
    bias_out[...] = (tail[:, :SHARD] - LEARN_RATE * bias_grad * lax.rsqrt(bias_sums)).astype(BF16)


def shards(
    row_factors,
    row_bias,
    row_sums,
    row_bias_sums,
    col_factors,
    col_bias,
    col_sums,
    col_bias_sums,
    row_pick,
    counts,
):
    at = lax.axis_index("group")
    y = (at % NY).astype(jnp.int32).reshape(1)
    way = 1 - 2 * (lax.axis_index("stratum") % 2)
    ids = ((at // NY + way * jnp.arange(NZ) + NZ) % NZ).astype(jnp.int32)

    own_shard = pack(col_factors, col_bias)
    other_shard = swap_y(own_shard)
    pick_row = row_pick[0, 0]
    table, bias, sums, bias_sums = (
        row_factors,
        row_bias.reshape(1, RTAB),
        row_sums,
        row_bias_sums.reshape(1, RTAB),
    )
    picked = gather(table, bias, pick_row)
    own = merge(y, own_shard, other_shard, (picked[0],))
    columns = gather_columns(own)

    part, grads, near_grad = step_tiles(0, ids, picked, columns, counts)
    held = call(hold_kernel, HELD, n_in=4, n_after=1)(
        col_factors, col_bias.reshape(1, SHARD), col_sums, col_bias_sums.reshape(1, SHARD), near_grad
    )
    held = (next_stratum(held), next_stratum_swap_y(held))
    table, bias, sums, bias_sums, *picked = row_update(
        0, False, *grads, table, bias, sums, bias_sums, pick_row
    )
    total = call(sum_kernel, CODED, size=1 << 20, n_in=5)(*reduce_columns(part, (picked[0], *held)))
    own, block_sums = call(
        column_update_kernel,
        (shape((PIECE_B, K), BF16), shape((PIECE_F, K), F32)),
        size=2 << 20,
        specs=[SMEM] + [VMEM] * 4,
    )(y, next_stratum(total), next_stratum_swap_y(total), *held)

    columns = gather_columns(own)
    part, grads, near_grad = step_tiles(1, ids, picked, columns, counts)
    held = call(hold_half_kernel, HELD, specs=[SMEM] + [VMEM] * 2, n_after=1)(
        y, own, block_sums, near_grad
    )
    held = next_stratum(held)
    table, bias, sums, bias_sums = row_update(
        1, True, *grads, table, bias, sums, bias_sums, pick_row
    )
    mine, theirs = call(
        split_sum_kernel,
        (CODED_HALF, CODED_HALF),
        size=1 << 20,
        specs=[SMEM] + [VMEM] * 5,
    )(y, *reduce_columns(part, (bias, held)))
    new_block, new_bias, new_sums, new_bias_sums = call(
        last_update_kernel,
        (
            shape((SHARD, K), BF16),
            shape((1, SHARD), BF16),
            shape((SHARD, K), F32),
            shape((1, SHARD), F32),
        ),
        size=1 << 20,
        specs=[SMEM] + [VMEM] * 3,
    )(y, next_stratum(mine), next_stratum_swap_y(theirs), held)
    return (
        table,
        bias.reshape(RTAB),
        sums,
        bias_sums.reshape(RTAB),
        new_block,
        new_bias.reshape(SHARD),
        new_sums,
        new_bias_sums.reshape(SHARD),
    )


def solution(mesh):
    both = P(("stratum", "group"))
    rows = P(("stratum", "group"), None)
    in_specs = (
        rows,
        both,
        rows,
        both,
        rows,
        both,
        rows,
        both,
        P("stratum", "group", None, None),
        P("stratum", "group", None, None, None),
    )
    out_specs = (rows, both, rows, both, rows, both, rows, both)
    return jax.shard_map(shards, mesh=mesh, in_specs=in_specs, out_specs=out_specs, check_vma=False)
```
